512 devices in a mesh: tm: 64 (over x, z), row: 8 (over y, core).
Axes of the slice: x: 4, y: 4, z: 16, core: 2. Of those that a mesh axis runs over, the one named last changes fastest.
Arguments:
- observations: bfloat16 [256, 128], P('tm'), may hold values from -6 to 6
- gain: bfloat16 [1024, 128], replicated, may hold values from -1 to 1
- damping: float32 [256, 1024], P('tm'), may hold values from 0.4 to 1
- blocks: bfloat16 [256, 1024, 128], P('tm', 'row'), may hold values from -0.109375 to 0.109375
- pattern: int32 [64, 8], replicated, may hold values from 0 to 63, as said below
- sensor_index: int32 [128], replicated, may hold values from 0 to 1023, as said below
Outputs:
- element_matrix: bfloat16 [64, 1024, 1024], P('tm', 'row')
- element_vector: float32 [64, 1024], P('tm', 'row')
The draws below stay inside these ranges and needn't reach their ends.
Inputs may be any that keep to these rules, and one draw needn't show every extreme that they name: `pattern`: each block row names 8 different block columns. `sensor_index`: the sensors observe different states.
All inputs are finite; a program needn't handle non-finite values.
Results may differ from the reference program's by a relative error of at most 0.035.
Values may be sent and summed in bfloat16 or wider, within the bound.
A program may use at most 64 MiB of HBM per device.

```python
import jax
import jax.numpy as jnp
from jax import lax

STATES = 1024
SENSORS = 128
BS = 16
S = 8
STRETCH = 4
LEVELS = 4
NBLK = 64
EPOCH_COUNT = 256
N_TM = 64


def sensor_states(key):
    return jax.random.permutation(key, STATES)[:SENSORS].astype(jnp.int32)


def draw_sensor_index(key, part):
    return sensor_states(key)


def draw_gain(key, part):
    chosen = sensor_states(key)
    key = jax.random.fold_in(key, 41)
    key_fill, key_level = jax.random.split(key, 2)
    fill = jnp.clip(jax.random.normal(key_fill, (STATES, SENSORS), jnp.float32), -4.0, 4.0)
    level = 0.25 + 0.5 * jax.random.uniform(key_level, (1, SENSORS), jnp.float32)
    match = (jnp.arange(STATES, dtype=jnp.int32)[:, None] == chosen[None, :]).astype(jnp.float32)
    observed_row = jnp.max(match, axis=1, keepdims=True)
    spread = (0.4 - 0.25 * observed_row) / jnp.sqrt(jnp.float32(SENSORS))
    return (fill * spread + match * level).astype(jnp.bfloat16)


def draw_damping(key, part):
    key = jax.random.fold_in(key, 11)
    seed_speed_draw, seed_surface_friction, seed_sudden_disturbance, seed_seabed_level = jax.random.split(key, 4)
    low = 1.0 / (4.0 * EPOCH_COUNT)
    high = 1.0 / 30.0
    spread = jax.random.uniform(seed_speed_draw, (1, STATES), jnp.float32)
    rate = jnp.exp(jnp.log(low) + spread * (jnp.log(high) - jnp.log(low)))
    rough = 0.5 + jax.random.uniform(seed_surface_friction, (EPOCH_COUNT, STATES), jnp.float32)
    sudden_disturbance = jax.random.randint(seed_sudden_disturbance, (EPOCH_COUNT, 1), 0, EPOCH_COUNT) < 4
    seabed_distance = 0.5 + 0.3 * jax.random.uniform(seed_seabed_level, (EPOCH_COUNT, 1), jnp.float32)
    magnitude_multiplier = jnp.where(sudden_disturbance, seabed_distance, jnp.ones_like(seabed_distance))
    return jnp.exp(-rate * rough) * magnitude_multiplier


def draw_pattern(key, part):
    key = jax.random.fold_in(key, 23)
    row_keys = jax.random.split(key, NBLK)

    def one_row(row_key):
        return jax.random.permutation(row_key, NBLK)[:S]
    return jax.vmap(one_row)(row_keys).astype(jnp.int32)


def block_scale(own_key, shape, shards, low, high):
    level = 1.0
    for axis_at, blocks in shards:
        heights = jax.random.uniform(jax.random.fold_in(jax.random.fold_in(own_key, 6), axis_at), (blocks,), jnp.float32, low / len(shards), high / len(shards))
        level = level * jnp.repeat(jnp.exp(heights), shape[axis_at] // blocks).reshape((-1,) + (1,) * (len(shape) - 1 - axis_at))
    return level


def centred(stream_key, dims, scale, limit, pieces=(), kind=jnp.bfloat16):
    values = scale * jax.random.normal(stream_key, dims, jnp.float32)
    if pieces:
        values = values * block_scale(stream_key, dims, pieces, -0.22, 0.18)
    return jnp.clip(values, -limit, limit).astype(kind)


def setup_inputs(seed: int = 0) -> dict:
    key_of = jax.random.split(jax.random.key(seed), 7)
    return {
        "observations": centred(key_of[0], (EPOCH_COUNT, SENSORS), 1.0, 6.0, ((0, 64),)),
        "gain": draw_gain(jax.random.fold_in(key_of[6], 71), 0),
        "damping": draw_damping(jax.random.fold_in(key_of[6], 71), 0),
        "blocks": centred(key_of[3], (EPOCH_COUNT, STATES, S * BS), (25 * S * BS) ** -0.5, 0.109375, ((0, 64), (1, 8))),
        "pattern": draw_pattern(jax.random.fold_in(key_of[6], 71), 0),
        "sensor_index": draw_sensor_index(jax.random.fold_in(key_of[6], 71), 0),
    }


def sparse_product(weighted, step_blocks, pattern):
    left = weighted.astype(jnp.float32).reshape(STATES, NBLK, BS)
    right = step_blocks.astype(jnp.float32).reshape(NBLK, BS, S, BS)
    partial_value = jnp.einsum('irk,rksl->irsl', left, right, precision=lax.Precision.HIGHEST)
    result = jnp.zeros((STATES, NBLK, BS), jnp.float32)
    result = result.at[:, pattern.reshape(-1)].add(partial_value.reshape(STATES, NBLK * S, BS))
    return result.reshape(STATES, STATES)


def stretch_element(obs_block, damp_block, block_values, gain, pattern, sensor_index):
    innovation = jnp.dot(obs_block, gain.T, preferred_element_type=jnp.float32)
    carry = jnp.eye(STATES, dtype=jnp.float32)
    offset = jnp.zeros((STATES,), jnp.float32)
    gain_wide = gain.astype(jnp.float32)
    for step in reversed(range(STRETCH)):
        offset = offset + jnp.dot(carry, innovation[step], precision=lax.Precision.HIGHEST)
        through_gain = jnp.dot(carry, gain_wide, precision=lax.Precision.HIGHEST)
        projected = carry.at[:, sensor_index].add(-through_gain)
        weighted = projected.astype(jnp.bfloat16)
        carry = weighted.astype(jnp.float32) * damp_block[step][None, :] + sparse_product(weighted, block_values[step], pattern)
    return carry.astype(jnp.bfloat16), offset


def reference(observations, gain, damping, blocks, pattern, sensor_index):
    obs_all = observations.reshape(N_TM, STRETCH, SENSORS)
    damp_all = damping.reshape(N_TM, STRETCH, STATES)
    block_all = blocks.reshape(N_TM, STRETCH, STATES, S * BS)

    def build(items):
        return stretch_element(items[0], items[1], items[2], gain, pattern, sensor_index)

    matrices, vectors = lax.map(build, (obs_all, damp_all, block_all))
    for level in range(LEVELS):
        span = 2 ** level
        later_idx = jnp.arange(2 * span - 1, N_TM, 2 * span, dtype=jnp.int32)
        earlier_idx = later_idx - span
        later = matrices[later_idx].astype(jnp.float32)
        earlier = matrices[earlier_idx].astype(jnp.float32)
        new_vectors = jnp.einsum('cij,cj->ci', later, vectors[earlier_idx], precision=lax.Precision.HIGHEST) + vectors[later_idx]
        new_matrices = jnp.einsum('cij,cjk->cik', later, earlier, precision=lax.Precision.HIGHEST).astype(jnp.bfloat16)
        matrices = matrices.at[later_idx].set(new_matrices)
        vectors = vectors.at[later_idx].set(new_vectors)
    return matrices, vectors
```

```python
import functools

import jax
import jax.numpy as jnp
from jax import lax
from jax.experimental import pallas as pl
from jax.experimental.pallas import tpu as pltpu
from jax.sharding import PartitionSpec as P

STATES = 1024
SENSORS = 128
BS = 16
S = 8
STRETCH = 4
NBLK = 64
GROUP = 8
ROWS = STATES // GROUP
STEPS = 2 * STRETCH
CHUNK = 256
PARTS = STATES // CHUNK
SPANS = (2, 4, 8)
MESH = pl.DeviceIdType.MESH
F32 = jnp.float32
BF16 = jnp.bfloat16


def dot(a, b):
    return jnp.dot(a, b, preferred_element_type=F32)


def iota(shape, axis):
    return lax.broadcasted_iota(jnp.int32, shape, axis)


def kernel(
    pattern, sensor, observations, gain, damping, blocks,
    matrix_out, vector_out,
    comp, small, damp_wide, obs_wide, pick, state, mixed, mixed_b, vector_f,
    saved, saved_v, rows_of, parts_in, vec_in, vec_row, vec_send,
    in_sem, pair_send, pair_recv, small_send, small_recv,
    c_send, c_left, c_right, c_half, c_core,
    p_send, p_left, p_right, p_half, p_core, p_in,
    swap_send, swap_recv, direct_send, up_send, vec_sends, vec_recv, out_sem,
):
    t = lax.axis_index("tm")
    i = lax.axis_index("row")
    core = i % 2
    y = i // 2
    above = ((y + 1) % 4) * 2 + core
    below = ((y + 3) % 4) * 2 + core
    opposite = ((y + 2) % 4) * 2 + core
    twin = i + 1 - 2 * core
    odd = t % 2
    pair = t + 1 - 2 * odd
    producer = [t % (2 * span) == span - 1 for span in SPANS]
    consumer = [t % (2 * span) == 2 * span - 1 for span in SPANS]
    merges = sum(c.astype(jnp.int32) for c in consumer)
    meets = merges + sum(p.astype(jnp.int32) for p in producer)

    def send(src, dst, send_sem, recv_sem, device):
        pltpu.make_async_remote_copy(
            src_ref=src, dst_ref=dst, send_sem=send_sem, recv_sem=recv_sem,
            device_id=device, device_id_type=MESH,
        ).start()

    def await_bytes(ref, sem):
        pltpu.make_async_copy(ref, ref, sem).wait()

    own_rows = pl.ds(pl.multiple_of(i * ROWS, ROWS), ROWS)
    fetch = pltpu.make_async_copy(
        blocks, comp.at[pl.ds(odd * STRETCH, STRETCH), own_rows, :], in_sem
    )
    fetch.start()

    barrier = pltpu.get_barrier_semaphore()

    def greet(device):
        pl.semaphore_signal(barrier, inc=1, device_id=device, device_id_type=MESH)

    greet((pair, i))
    for d in range(1, GROUP):
        greet((t, (i + d) % GROUP))
    for at, span in enumerate(SPANS):
        @pl.when(producer[at])
        def _():
            for j in range(GROUP):
                greet((t + span, j))

        @pl.when(consumer[at])
        def _():
            for j in range(GROUP):
                greet((t - span, j))

    small[odd] = jnp.zeros((8, STATES), F32)
    small[odd, 0:STRETCH, :] = damping[...]
    small[odd, STRETCH:8, 0:SENSORS] = observations[...].astype(F32)
    eye = iota((SENSORS, SENSORS), 0) == iota((SENSORS, SENSORS), 1)
    sensor_col = jnp.sum(
        jnp.where(eye, jnp.broadcast_to(sensor[...].astype(F32), (SENSORS, SENSORS)), 0.0),
        axis=1, keepdims=True,
    )
    pick[...] = jnp.where(
        sensor_col == iota((SENSORS, STATES), 1).astype(F32), 1.0, 0.0
    ).astype(BF16)
    first = iota((STATES, 2 * ROWS), 0) == iota((STATES, 2 * ROWS), 1) + i * ROWS
    state[...] = jnp.where(
        first & (iota((STATES, 2 * ROWS), 1) < ROWS), 1.0, 0.0
    ).astype(BF16).reshape(NBLK, BS, 2 * ROWS)
    pl.semaphore_wait(barrier, GROUP + GROUP * meets)

    def ring(buf, s_send, s_left, s_right, s_half, s_core):
        def piece(m, p, start=0, count=ROWS):
            return buf.at[m, pl.ds(pl.multiple_of(p * ROWS + start, 16), count), :]

        def begin(m):
            mine = piece(m, i)
            send(mine, mine, s_send.at[m], s_left.at[m], (t, above))
            send(mine, mine, s_send.at[m], s_right.at[m], (t, below))
            send(mine, mine, s_send.at[m], s_core.at[m], (t, twin))

        def forward(m):
            left = piece(m, below)
            await_bytes(left, s_left.at[m])
            half = piece(m, below, 0, ROWS // 2)
            send(half, half, s_send.at[m], s_half.at[m], (t, above))
            send(left, left, s_send.at[m], s_core.at[m], (t, twin))
            right = piece(m, above)
            await_bytes(right, s_right.at[m])
            half = piece(m, above, ROWS // 2, ROWS // 2)
            send(half, half, s_send.at[m], s_half.at[m], (t, below))
            send(right, right, s_send.at[m], s_core.at[m], (t, twin))

        def finish(m):
            far = piece(m, opposite)
            await_bytes(far, s_half.at[m])
            send(far, far, s_send.at[m], s_core.at[m], (t, twin))
            await_bytes(buf.at[m, pl.ds(0, 4 * ROWS), :], s_core.at[m])

        def drain(m):
            await_bytes(buf.at[m, pl.ds(0, 7 * ROWS), :], s_send.at[m])

        return begin, forward, finish, drain

    begin_c, forward_c, finish_c, drain_c = ring(comp, c_send, c_left, c_right, c_half, c_core)
    begin_p, forward_p, finish_p, drain_p = ring(parts_in, p_send, p_left, p_right, p_half, p_core)

    def start_step(n):
        @pl.when(n // STRETCH != odd)
        def _():
            await_bytes(comp.at[n, own_rows, :], pair_recv.at[n])

        begin_c(n)

    def widen(b):
        columns = jnp.transpose(small[b])
        for k in range(STRETCH):
            damp_wide[b * STRETCH + k] = jnp.broadcast_to(columns[:, k : k + 1], (STATES, ROWS))
            obs_wide[b * STRETCH + k] = jnp.broadcast_to(
                columns[:SENSORS, STRETCH + k : STRETCH + k + 1], (SENSORS, ROWS)
            )

    send(small.at[odd], small.at[odd], small_send, small_recv, (pair, i))
    fetch.wait()

    def give(k, carry):
        ref = comp.at[odd * STRETCH + k, own_rows, :]
        send(ref, ref, pair_send.at[k], pair_recv.at[odd * STRETCH + k], (pair, i))
        return carry

    lax.fori_loop(0, STRETCH, give, 0)
    start_step(0)
    start_step(1)
    widen(odd)
    start_step(2)
    start_step(3)
    forward_c(0)
    await_bytes(small.at[1 - odd], small_recv)
    widen(1 - odd)
    forward_c(1)

    def step(n, carry):
        @pl.when(n + 4 < STEPS)
        def _():
            start_step(n + 4)

        @pl.when(n + 2 < STEPS)
        def _():
            forward_c(n + 2)

        finish_c(n)
        for part in range(GROUP):
            rows = slice(part * ROWS, (part + 1) * ROWS)
            products = []
            for r in range(part * GROUP, (part + 1) * GROUP):
                chosen = jnp.concatenate(
                    [
                        state[pattern[r, s]] for s in range(S)
                    ],
                    axis=0,
                )
                products.append(dot(comp[n, r * BS : (r + 1) * BS, :], chosen))
            wide = damp_wide[n, rows, :]
            value = state[part * GROUP : (part + 1) * GROUP].reshape(ROWS, 2 * ROWS).astype(F32) * jnp.concatenate([wide, wide], axis=1)
            value = value + jnp.concatenate(products, axis=0)
            mixed[rows, :] = value
            mixed_b[rows, :] = value.astype(BF16)
        quarter = STATES // 4
        seen = sum(
            dot(pick[:, q * quarter : (q + 1) * quarter], mixed_b[q * quarter : (q + 1) * quarter, :])
            for q in range(4)
        )
        lane = iota((SENSORS, ROWS), 1)
        readings = jnp.where(lane == 0, obs_wide[n], 0.0)
        seen = jnp.concatenate([seen[:, :ROWS], seen[:, ROWS:] - readings], axis=1).astype(BF16)
        for q in range(4):
            rows = slice(q * quarter, (q + 1) * quarter)
            value = mixed[rows, :] - dot(gain[rows, :], seen)
            state[q * 16 : (q + 1) * 16] = value.astype(BF16).reshape(16, BS, 2 * ROWS)
            vector_f[rows, :] = value[:, ROWS:]

        @pl.when(n == (1 + odd) * STRETCH - 1)
        def _():
            saved[...] = state[:, :, 0:ROWS].reshape(STATES, ROWS)
            saved_v[...] = vector_f[own_rows, :]

        return carry

    lax.fori_loop(0, STEPS, step, 0)

    def block(j):
        return saved.at[pl.ds(pl.multiple_of(j * ROWS, ROWS), ROWS), :]

    own_columns = pl.ds(pl.multiple_of(i * ROWS, ROWS), ROWS)

    @pl.when(producer[0])
    def _():
        lanes = pl.ds(pl.multiple_of((i % 2) * ROWS, ROWS), ROWS)
        for d in range(GROUP):
            j = (i + d) % GROUP
            rows = pl.ds(pl.multiple_of(j * ROWS, ROWS), ROWS)
            send(
                block(j), parts_in.at[i // 2, rows, lanes], direct_send, p_in.at[i // 2],
                (t + SPANS[0], j),
            )

    for d in range(1, GROUP):
        j = (i + d) % GROUP
        send(block(j), rows_of.at[0, :, own_columns], swap_send, swap_recv, (t, j))
    rows_of[0, :, own_columns] = saved[own_rows, :]
    vec_row[...] = jnp.transpose(saved_v[...])[0:8, :]

    def give_vector(level):
        value = vec_row[0:1, :]
        high = value.astype(BF16)
        low = (value - high.astype(F32)).astype(BF16)
        row = iota((16, ROWS), 0)
        both = jnp.where(
            row == 0, jnp.broadcast_to(high.astype(F32), (16, ROWS)),
            jnp.where(row == 1, jnp.broadcast_to(low.astype(F32), (16, ROWS)), 0.0),
        )
        vec_send[level] = both.astype(BF16)
        for j in range(GROUP):
            send(
                vec_send.at[level], vec_in.at[level, :, own_columns],
                vec_sends.at[level], vec_recv.at[level], (t + SPANS[level], j),
            )

    @pl.when(producer[0])
    def _():
        give_vector(0)

    def start_part(m):
        await_bytes(parts_in.at[m, own_rows, :], p_in.at[m])
        begin_p(m)

    count = PARTS * merges

    @pl.when(merges > 0)
    def _():
        start_part(0)
        start_part(1)
        forward_p(0)

    await_bytes(rows_of.at[0, :, pl.ds(0, 7 * ROWS)], swap_recv)

    def merge(m, carry):
        @pl.when(m + 2 < count)
        def _():
            start_part(m + 2)

        @pl.when(m + 1 < count)
        def _():
            forward_p(m + 1)

        finish_p(m)
        level = m // PARTS
        part = m % PARTS
        columns = pl.ds(pl.multiple_of(part * CHUNK, CHUNK), CHUNK)
        rows_of[level + 1, :, columns] = dot(rows_of[level], parts_in[m]).astype(BF16)
        for at in (1, 2):
            @pl.when(producer[at] & (level == at - 1))
            def _():
                send(
                    rows_of.at[level + 1, :, columns], parts_in.at[m + PARTS, own_rows, :],
                    up_send.at[part], p_in.at[m + PARTS], (t + SPANS[at], i),
                )

        @pl.when(part == 1)
        def _():
            await_bytes(vec_in.at[level], vec_recv.at[level])
            found = lax.dot_general(
                vec_in[level], rows_of[level], (((1,), (1,)), ((), ())),
                preferred_element_type=F32,
            )
            vec_row[0:1, :] = vec_row[0:1, :] + found[0:1, :] + found[1:2, :]
            for at in (1, 2):
                @pl.when(producer[at] & (level == at - 1))
                def _():
                    give_vector(at)

        return carry

    lax.fori_loop(0, count, merge, 0)

    result = pltpu.make_async_copy(rows_of.at[merges], matrix_out.at[0], out_sem)
    result.start()
    vector_out[...] = vec_row[0:1, :]

    def drained(n, carry):
        drain_c(n)
        return carry

    lax.fori_loop(0, STEPS, drained, 0)

    def given(k, carry):
        await_bytes(comp.at[odd * STRETCH + k, own_rows, :], pair_send.at[k])
        return carry

    lax.fori_loop(0, STRETCH, given, 0)
    await_bytes(small.at[odd], small_send)
    await_bytes(rows_of.at[0, :, pl.ds(0, 7 * ROWS)], swap_send)

    def drained_part(m, carry):
        drain_p(m)
        return carry

    lax.fori_loop(0, count, drained_part, 0)

    @pl.when(producer[0])
    def _():
        await_bytes(saved, direct_send)

    @pl.when(producer[1] | producer[2])
    def _():
        for part in range(PARTS):
            await_bytes(parts_in.at[0, own_rows, :], up_send.at[part])

    for at in range(3):
        @pl.when(producer[at])
        def _():
            await_bytes(vec_in.at[at], vec_sends.at[at])

    result.wait()


def shards(observations, gain, damping, blocks, pattern, sensor_index):
    vmem = pl.BlockSpec(memory_space=pltpu.VMEM)
    dma = pltpu.SemaphoreType.DMA
    merges = len(SPANS)
    moves = PARTS * merges
    return pl.pallas_call(
        kernel,
        out_shape=(
            jax.ShapeDtypeStruct((1, ROWS, STATES), BF16),
            jax.ShapeDtypeStruct((1, ROWS), F32),
        ),
        in_specs=[
            pl.BlockSpec(memory_space=pltpu.SMEM), vmem, vmem, vmem, vmem,
            pl.BlockSpec(memory_space=pl.ANY),
        ],
        out_specs=(pl.BlockSpec(memory_space=pl.ANY), vmem),
        scratch_shapes=[
            pltpu.VMEM((STEPS, STATES, SENSORS), BF16),
            pltpu.VMEM((2, 8, STATES), F32),
            pltpu.VMEM((STEPS, STATES, ROWS), F32),
            pltpu.VMEM((STEPS, SENSORS, ROWS), F32),
            pltpu.VMEM((SENSORS, STATES), BF16),
            pltpu.VMEM((NBLK, BS, 2 * ROWS), BF16),
            pltpu.VMEM((STATES, 2 * ROWS), F32),
            pltpu.VMEM((STATES, 2 * ROWS), BF16),
            pltpu.VMEM((STATES, ROWS), F32),
            pltpu.VMEM((STATES, ROWS), BF16),
            pltpu.VMEM((ROWS, ROWS), F32),
            pltpu.VMEM((merges + 1, ROWS, STATES), BF16),
            pltpu.VMEM((moves, STATES, CHUNK), BF16),
            pltpu.VMEM((merges, 16, STATES), BF16),
            pltpu.VMEM((8, ROWS), F32),
            pltpu.VMEM((merges, 16, ROWS), BF16),
            dma, dma((STRETCH,)), dma((STEPS,)), dma, dma,
            dma((STEPS,)), dma((STEPS,)), dma((STEPS,)), dma((STEPS,)), dma((STEPS,)),
            dma((moves,)), dma((moves,)), dma((moves,)), dma((moves,)), dma((moves,)), dma((moves,)),
            dma, dma, dma, dma((PARTS,)), dma((merges,)), dma((merges,)), dma,
        ],
        compiler_params=pltpu.CompilerParams(
            collective_id=0, has_side_effects=True, vmem_limit_bytes=48 * 2**20
        ),
    )(pattern, sensor_index.reshape(1, SENSORS), observations, gain, damping, blocks)


def solution(mesh):
    return jax.shard_map(
        shards,
        mesh=mesh,
        in_specs=(P("tm", None), P(), P("tm", None), P("tm", "row", None), P(), P()),
        out_specs=(P("tm", "row", None), P("tm", "row")),
        check_vma=False,
    )
```

```python
import functools

import jax
import jax.numpy as jnp
from jax import lax
from jax.experimental import pallas as pl
from jax.experimental.pallas import tpu as pltpu
from jax.sharding import PartitionSpec as P

STATES = 1024
SENSORS = 128
BS = 16
S = 8
STRETCH = 4
NBLK = 64
GROUP = 8
ROWS = STATES // GROUP
STEPS = 2 * STRETCH
CHUNK = 256
PARTS = STATES // CHUNK
SPANS = (2, 4, 8)
MESH = pl.DeviceIdType.MESH
F32 = jnp.float32
BF16 = jnp.bfloat16


def dot(a, b):
    return jnp.dot(a, b, preferred_element_type=F32)


def iota(shape, axis):
    return lax.broadcasted_iota(jnp.int32, shape, axis)


def kernel(
    pattern, sensor, observations, gain, damping, blocks,
    matrix_out, vector_out,
    comp, small, damp_wide, obs_wide, pick, state, mixed, mixed_b, vector_f,
    columns_of, whole, earlier, vec_in, vec_row, vec_send, rows_out,
    in_sem, small_send, small_recv,
    c_send, c_twin, c_mine, c_left, c_right, c_far, c_core,
    m_send, m_twin, m_left, m_right, m_far, m_core,
    up_send, up_recv, vec_sends, vec_recv, swap_send, swap_recv, out_sem,
):
    t = lax.axis_index("tm")
    i = lax.axis_index("row")
    core = i % 2
    y = i // 2
    above = ((y + 1) % 4) * 2 + core
    below = ((y + 3) % 4) * 2 + core
    opposite = ((y + 2) % 4) * 2 + core
    twin = i + 1 - 2 * core
    odd = t % 2
    pair = t + 1 - 2 * odd
    producer = [t % (2 * span) == span - 1 for span in SPANS]
    consumer = [t % (2 * span) == 2 * span - 1 for span in SPANS]
    merges = sum(c.astype(jnp.int32) for c in consumer)
    meets = merges + sum(p.astype(jnp.int32) for p in producer)
    count = PARTS * merges

    def send(src, dst, send_sem, recv_sem, device):
        pltpu.make_async_remote_copy(
            src_ref=src, dst_ref=dst, send_sem=send_sem, recv_sem=recv_sem,
            device_id=device, device_id_type=MESH,
        ).start()

    def await_bytes(ref, sem):
        pltpu.make_async_copy(ref, ref, sem).wait()

    def span_of(p, size=ROWS):
        return pl.ds(pl.multiple_of(p * size, size), size)

    own = span_of(i)
    fetch = pltpu.make_async_copy(
        blocks, comp.at[pl.ds(odd * STRETCH, STRETCH), own, :], in_sem
    )
    fetch.start()

    barrier = pltpu.get_barrier_semaphore()

    def greet(device):
        pl.semaphore_signal(barrier, inc=1, device_id=device, device_id_type=MESH)

    for j in (i, above, below, opposite):
        greet((pair, j))
    for d in range(1, GROUP):
        greet((t, (i + d) % GROUP))
    for at, span in enumerate(SPANS):
        @pl.when(producer[at])
        def _():
            greet((t + span, i))

        @pl.when(consumer[at])
        def _():
            greet((t - span, i))

    small[odd] = jnp.zeros((8, STATES), F32)
    small[odd, 0:STRETCH, :] = damping[...]
    small[odd, STRETCH:8, 0:SENSORS] = observations[...].astype(F32)
    eye = iota((SENSORS, SENSORS), 0) == iota((SENSORS, SENSORS), 1)
    sensor_col = jnp.sum(
        jnp.where(eye, jnp.broadcast_to(sensor[...].astype(F32), (SENSORS, SENSORS)), 0.0),
        axis=1, keepdims=True,
    )
    pick[...] = jnp.where(
        sensor_col == iota((SENSORS, STATES), 1).astype(F32), 1.0, 0.0
    ).astype(BF16)
    first = iota((STATES, 2 * ROWS), 0) == iota((STATES, 2 * ROWS), 1) + i * ROWS
    state[...] = jnp.where(
        first & (iota((STATES, 2 * ROWS), 1) < ROWS), 1.0, 0.0
    ).astype(BF16).reshape(NBLK, BS, 2 * ROWS)
    pl.semaphore_wait(barrier, GROUP + 3 + meets)

    def piece(n, p):
        return comp.at[n, span_of(p), :]

    def give_step(n):
        mine = piece(n, i)
        for group in (t, pair):
            send(mine, mine, c_send.at[n], c_far.at[n], (group, opposite))
            send(mine, mine, c_send.at[n], c_left.at[n], (group, above))
            send(mine, mine, c_send.at[n], c_right.at[n], (group, below))
        send(mine, mine, c_send.at[n], c_mine.at[n], (pair, i))
        send(mine, mine, c_twin.at[n], c_core.at[n], (t, twin))

    def pass_step(n):
        @pl.when(n // STRETCH != odd)
        def _():
            mine = piece(n, i)
            await_bytes(mine, c_mine.at[n])
            send(mine, mine, c_twin.at[n], c_core.at[n], (t, twin))

        for p, sems in ((below, c_left), (above, c_right), (opposite, c_far)):
            part = piece(n, p)
            await_bytes(part, sems.at[n])
            send(part, part, c_twin.at[n], c_core.at[n], (t, twin))

    def widen(b):
        columns = jnp.transpose(small[b])
        for k in range(STRETCH):
            damp_wide[b * STRETCH + k] = jnp.broadcast_to(columns[:, k : k + 1], (STATES, ROWS))
            obs_wide[b * STRETCH + k] = jnp.broadcast_to(
                columns[:SENSORS, STRETCH + k : STRETCH + k + 1], (SENSORS, ROWS)
            )

    fetch.wait()

    @pl.when(odd == 0)
    def _():
        give_step(0)

    send(small.at[odd], small.at[odd], small_send, small_recv, (pair, i))

    @pl.when(odd == 0)
    def _():
        def give(k, carry):
            give_step(k)
            return carry

        lax.fori_loop(1, STRETCH, give, 0)

    widen(odd)
    await_bytes(small.at[1 - odd], small_recv)
    widen(1 - odd)
    pass_step(0)

    @pl.when(odd == 1)
    def _():
        give_step(STRETCH)

    def step(n, carry):
        @pl.when((odd == 1) & (n < STRETCH - 1))
        def _():
            give_step(n + STRETCH + 1)

        @pl.when(n + 1 < STEPS)
        def _():
            pass_step(n + 1)

        await_bytes(comp.at[n, pl.ds(0, 4 * ROWS), :], c_core.at[n])
        for part in range(GROUP):
            rows = slice(part * ROWS, (part + 1) * ROWS)
            products = []
            for r in range(part * GROUP, (part + 1) * GROUP):
                chosen = jnp.concatenate([state[pattern[r, s]] for s in range(S)], axis=0)
                products.append(dot(comp[n, r * BS : (r + 1) * BS, :], chosen))
            wide = damp_wide[n, rows, :]
            old = state[part * GROUP : (part + 1) * GROUP].reshape(ROWS, 2 * ROWS)
            value = old.astype(F32) * jnp.concatenate([wide, wide], axis=1)
            value = value + jnp.concatenate(products, axis=0)
            mixed[rows, :] = value
            mixed_b[rows, :] = value.astype(BF16)
        quarter = STATES // 4
        seen = sum(
            dot(pick[:, q * quarter : (q + 1) * quarter], mixed_b[q * quarter : (q + 1) * quarter, :])
            for q in range(4)
        )
        lane = iota((SENSORS, ROWS), 1)
        readings = jnp.where(lane == 0, obs_wide[n], 0.0)
        seen = jnp.concatenate([seen[:, :ROWS], seen[:, ROWS:] - readings], axis=1).astype(BF16)
        for q in range(4):
            rows = slice(q * quarter, (q + 1) * quarter)
            value = mixed[rows, :] - dot(gain[rows, :], seen)
            state[q * 16 : (q + 1) * 16] = value.astype(BF16).reshape(16, BS, 2 * ROWS)
            vector_f[rows, :] = value[:, ROWS:]

        @pl.when(n == (1 + odd) * STRETCH - 1)
        def _():
            columns_of[0] = state[:, :, 0:ROWS].reshape(STATES, ROWS)
            for part in range(GROUP):
                rows = slice(part * ROWS, (part + 1) * ROWS)
                vec_row[0:1, rows] = jnp.transpose(vector_f[rows, :])[0:1, :]

        return carry

    lax.fori_loop(0, STEPS, step, 0)

    def rows_at(m):
        return span_of(m % PARTS, CHUNK)

    def give_vector(level):
        value = vec_row[0:1, :]
        high = value.astype(BF16).astype(F32)
        row = iota((16, STATES), 0)
        both = jnp.where(
            row == 0, jnp.broadcast_to(high, (16, STATES)),
            jnp.where(row == 1, jnp.broadcast_to(value - high, (16, STATES)), 0.0),
        )
        vec_send[...] = both.astype(BF16)
        send(vec_send, vec_in.at[level], vec_sends, vec_recv.at[level], (t + SPANS[level], i))

    def give_up(level, m):
        rows = rows_at(m)
        send(
            columns_of.at[level, rows, :], earlier.at[level, rows, :],
            up_send.at[m % PARTS], up_recv.at[level * PARTS + m % PARTS], (t + SPANS[level], i),
        )

    def give_part(m):
        level = m // PARTS
        rows = rows_at(m)
        src = columns_of.at[level, rows, :]
        dst = whole.at[level, rows, own]
        send(src, dst, m_send.at[m], m_far.at[m], (t, opposite))
        send(src, dst, m_send.at[m], m_left.at[m], (t, above))
        send(src, dst, m_send.at[m], m_right.at[m], (t, below))
        send(src, dst, m_twin.at[m], m_core.at[m], (t, twin))
        whole[level, rows, own] = columns_of[level, rows, :]

    def pass_part(m):
        for p, sems in ((below, m_left), (above, m_right), (opposite, m_far)):
            part = whole.at[m // PARTS, rows_at(m), span_of(p)]
            await_bytes(part, sems.at[m])
            send(part, part, m_twin.at[m], m_core.at[m], (t, twin))

    @pl.when(producer[0])
    def _():
        for m in range(PARTS):
            give_up(0, m)
        give_vector(0)

    @pl.when(merges > 0)
    def _():
        def give(m, carry):
            give_part(m)
            return carry

        lax.fori_loop(0, PARTS, give, 0)
        pass_part(0)

    def merge(m, carry):
        @pl.when(m + 1 < count)
        def _():
            pass_part(m + 1)

        level = m // PARTS
        rows = rows_at(m)

        @pl.when(m % PARTS == 0)
        def _():
            for q in range(PARTS):
                await_bytes(
                    earlier.at[level, pl.ds(q * CHUNK, CHUNK), :], up_recv.at[level * PARTS + q]
                )

        await_bytes(whole.at[level, rows, pl.ds(0, 4 * ROWS)], m_core.at[m])
        columns_of[level + 1, rows, :] = dot(whole[level, rows, :], earlier[level]).astype(BF16)

        @pl.when(m + PARTS < count)
        def _():
            give_part(m + PARTS)

        for at in (1, 2):
            @pl.when(producer[at] & (level == at - 1))
            def _():
                give_up(at, m)

        @pl.when(m % PARTS == PARTS - 1)
        def _():
            await_bytes(vec_in.at[level], vec_recv.at[level])
            found = lax.dot_general(
                vec_in[level], whole[level], (((1,), (1,)), ((), ())),
                preferred_element_type=F32,
            )
            vec_row[0:1, :] = vec_row[0:1, :] + found[0:1, :] + found[1:2, :]
            for at in (1, 2):
                @pl.when(producer[at] & (level == at - 1))
                def _():
                    give_vector(at)

        return carry

    lax.fori_loop(0, count, merge, 0)

    for d in (4, 5, 3, 2, 6, 7, 1):
        j = (i + d) % GROUP
        send(
            columns_of.at[merges, span_of(j), :], rows_out.at[:, own], swap_send, swap_recv, (t, j)
        )
    rows_out[:, own] = columns_of[merges, own, :]
    vector_out[...] = vec_row[0:1, own]

    def drained(n, carry):
        await_bytes(comp.at[n, pl.ds(0, 4 * ROWS), :], c_twin.at[n])
        return carry

    lax.fori_loop(0, STEPS, drained, 0)

    def drained_own(k, carry):
        n = odd * STRETCH + k
        await_bytes(comp.at[n, pl.ds(0, 7 * ROWS), :], c_send.at[n])
        return carry

    lax.fori_loop(0, STRETCH, drained_own, 0)
    await_bytes(small.at[odd], small_send)

    def drained_part(m, carry):
        rows = rows_at(m)
        await_bytes(whole.at[m // PARTS, rows, pl.ds(0, 3 * ROWS)], m_send.at[m])
        await_bytes(whole.at[m // PARTS, rows, pl.ds(0, 4 * ROWS)], m_twin.at[m])
        return carry

    lax.fori_loop(0, count, drained_part, 0)

    @pl.when(producer[0] | producer[1] | producer[2])
    def _():
        for q in range(PARTS):
            await_bytes(earlier.at[0, pl.ds(q * CHUNK, CHUNK), :], up_send.at[q])
        await_bytes(vec_send, vec_sends)

    await_bytes(rows_out.at[:, pl.ds(0, 7 * ROWS)], swap_recv)
    result = pltpu.make_async_copy(rows_out, matrix_out.at[0], out_sem)
    result.start()
    await_bytes(rows_out.at[:, pl.ds(0, 7 * ROWS)], swap_send)
    result.wait()


def shards(observations, gain, damping, blocks, pattern, sensor_index):
    vmem = pl.BlockSpec(memory_space=pltpu.VMEM)
    dma = pltpu.SemaphoreType.DMA
    merges = len(SPANS)
    moves = PARTS * merges
    return pl.pallas_call(
        kernel,
        out_shape=(
            jax.ShapeDtypeStruct((1, ROWS, STATES), BF16),
            jax.ShapeDtypeStruct((1, ROWS), F32),
        ),
        in_specs=[
            pl.BlockSpec(memory_space=pltpu.SMEM), vmem, vmem, vmem, vmem,
            pl.BlockSpec(memory_space=pl.ANY),
        ],
        out_specs=(pl.BlockSpec(memory_space=pl.ANY), vmem),
        scratch_shapes=[
            pltpu.VMEM((STEPS, STATES, SENSORS), BF16),
            pltpu.VMEM((2, 8, STATES), F32),
            pltpu.VMEM((STEPS, STATES, ROWS), F32),
            pltpu.VMEM((STEPS, SENSORS, ROWS), F32),
            pltpu.VMEM((SENSORS, STATES), BF16),
            pltpu.VMEM((NBLK, BS, 2 * ROWS), BF16),
            pltpu.VMEM((STATES, 2 * ROWS), F32),
            pltpu.VMEM((STATES, 2 * ROWS), BF16),
            pltpu.VMEM((STATES, ROWS), F32),
            pltpu.VMEM((merges + 1, STATES, ROWS), BF16),
            pltpu.VMEM((merges, STATES, STATES), BF16),
            pltpu.VMEM((merges, STATES, ROWS), BF16),
            pltpu.VMEM((merges, 16, STATES), BF16),
            pltpu.VMEM((8, STATES), F32),
            pltpu.VMEM((16, STATES), BF16),
            pltpu.VMEM((ROWS, STATES), BF16),
            dma, dma, dma,
            *[dma((STEPS,))] * 7,
            *[dma((moves,))] * 6,
            dma((PARTS,)), dma((moves,)), dma, dma((merges,)), dma, dma, dma,
        ],
        compiler_params=pltpu.CompilerParams(
            collective_id=0, has_side_effects=True, vmem_limit_bytes=48 * 2**20
        ),
    )(pattern, sensor_index.reshape(1, SENSORS), observations, gain, damping, blocks)


def solution(mesh):
    return jax.shard_map(
        shards,
        mesh=mesh,
        in_specs=(P("tm", None), P(), P("tm", None), P("tm", "row", None), P(), P()),
        out_specs=(P("tm", "row", None), P("tm", "row")),
        check_vma=False,
    )
```

```python
import functools

import jax
import jax.numpy as jnp
from jax import lax
from jax.experimental import pallas as pl
from jax.experimental.pallas import tpu as pltpu
from jax.sharding import PartitionSpec as P

STATES = 1024
SENSORS = 128
BS = 16
S = 8
STRETCH = 4
NBLK = 64
GROUP = 8
ROWS = STATES // GROUP
STEPS = 2 * STRETCH
CHUNK = 256
PARTS = STATES // CHUNK
PACE = 4
SPANS = (2, 4, 8)
VMEM_BYTES = 63 * 2**20
MESH = pl.DeviceIdType.MESH
F32 = jnp.float32
BF16 = jnp.bfloat16


def dot(a, b):
    return jnp.dot(a, b, preferred_element_type=F32)


def iota(shape, axis):
    return lax.broadcasted_iota(jnp.int32, shape, axis)


def kernel(
    pattern_in, sensor_in, observations_in, gain_in, damping_in, blocks,
    matrix_out, vector_out,
    pattern, sensor, observations, gain, damping,
    comp, small, damp_wide, obs_wide, pick, state, mixed, mixed_b, vector_f,
    columns_of, whole, earlier, vec_in, vec_row, vec_send, rows_out,
    in_sems, small_send, small_recv,
    c_send, c_over, c_twin, c_mine, c_left, c_right, c_far, c_core,
    m_send, m_twin, m_left, m_right, m_far, m_core,
    up_send, up_recv, vec_sends, vec_recv, swap_send, swap_recv, out_sem,
):
    t = lax.axis_index("tm")
    i = lax.axis_index("row")
    core = i % 2
    y = i // 2
    above = ((y + 1) % 4) * 2 + core
    below = ((y + 3) % 4) * 2 + core
    opposite = ((y + 2) % 4) * 2 + core
    twin = i + 1 - 2 * core
    odd = t % 2
    lead = t - odd + 1
    producer = [t % (2 * span) == span - 1 for span in SPANS]
    consumer = [t % (2 * span) == 2 * span - 1 for span in SPANS]
    merges = sum(c.astype(jnp.int32) for c in consumer)
    meets = sum(p.astype(jnp.int32) for p in producer)
    count = PARTS * merges

    def send(src, dst, send_sem, recv_sem, device):
        pltpu.make_async_remote_copy(
            src_ref=src, dst_ref=dst, send_sem=send_sem, recv_sem=recv_sem,
            device_id=device, device_id_type=MESH,
        ).start()

    def await_bytes(ref, sem):
        pltpu.make_async_copy(ref, ref, sem).wait()

    def span_of(p, size=ROWS):
        return pl.ds(pl.multiple_of(p * size, size), size)

    own = span_of(i)
    fetches = [
        pltpu.make_async_copy(src, dst, in_sems.at[k])
        for k, (src, dst) in enumerate(
            (
                (blocks, comp.at[pl.ds(odd * STRETCH, STRETCH), own, :]),
                (damping_in, damping), (observations_in, observations),
                (sensor_in, sensor), (pattern_in, pattern), (gain_in, gain),
            )
        )
    ]
    for fetch in fetches:
        fetch.start()
    barrier = pltpu.get_barrier_semaphore()

    def greet(device):
        pl.semaphore_signal(barrier, inc=1, device_id=device, device_id_type=MESH)

    for at, span in enumerate(SPANS):
        @pl.when(consumer[at])
        def _():
            greet((t - span, i))

    @pl.when(odd == 1)
    def _():
        greet((t - 1, i))

    for d in range(1, GROUP):
        greet((t, (i + d) % GROUP))

    for fetch in fetches[1:3]:
        fetch.wait()
    small[odd] = jnp.zeros((8, STATES), F32)
    small[odd, 0:STRETCH, :] = damping[...]
    small[odd, STRETCH:8, 0:SENSORS] = observations[...].astype(F32)
    for fetch in fetches[3:5]:
        fetch.wait()

    def widen(b):
        columns = jnp.transpose(small[b])
        for k in range(STRETCH):
            damp_wide[b * STRETCH + k] = jnp.broadcast_to(columns[:, k : k + 1], (STATES, ROWS))
            obs_wide[b * STRETCH + k] = jnp.broadcast_to(
                columns[:SENSORS, STRETCH + k : STRETCH + k + 1], (SENSORS, ROWS)
            )

    if True:
        eye = iota((SENSORS, SENSORS), 0) == iota((SENSORS, SENSORS), 1)
        sensor_col = jnp.sum(
            jnp.where(eye, jnp.broadcast_to(sensor[...].astype(F32), (SENSORS, SENSORS)), 0.0),
            axis=1, keepdims=True,
        )
        pick[...] = jnp.where(
            sensor_col == iota((SENSORS, STATES), 1).astype(F32), 1.0, 0.0
        ).astype(BF16)
        first = iota((STATES, 2 * ROWS), 0) == iota((STATES, 2 * ROWS), 1) + i * ROWS
        state[...] = jnp.where(
            first & (iota((STATES, 2 * ROWS), 1) < ROWS), 1.0, 0.0
        ).astype(BF16).reshape(NBLK, BS, 2 * ROWS)
        widen(odd)

    fetches[0].wait()
    fetches[5].wait()
    pl.semaphore_wait(barrier, GROUP - odd + meets)

    def piece(n, p):
        return comp.at[n, span_of(p), :]

    def give_step(n):
        mine = piece(n, i)
        send(mine, mine, c_twin.at[n], c_core.at[n], (t, twin))
        send(mine, mine, c_send.at[n], c_far.at[n], (t, opposite))
        send(mine, mine, c_send.at[n], c_left.at[n], (t, above))
        send(mine, mine, c_send.at[n], c_right.at[n], (t, below))

    def pass_step(n):
        for p, sems in ((below, c_left), (above, c_right), (opposite, c_far)):
            part = piece(n, p)
            await_bytes(part, sems.at[n])
            send(part, part, c_twin.at[n], c_core.at[n], (t, twin))

    def hand_over(k):
        ref = piece(k, i)
        send(ref, ref, c_over.at[k], c_mine.at[k], (lead, i))

    def own_rows_out():
        for d in (4, 5, 3, 2, 6, 7, 1):
            j = (i + d) % GROUP
            send(
                columns_of.at[0, span_of(j), :], rows_out.at[:, own], swap_send, swap_recv, (t, j)
            )
        rows_out[:, own] = columns_of[0, own, :]

    last_step = STRETCH * (1 + odd)

    def step(n, carry):
        @pl.when(n + 1 < last_step)
        def _():
            pass_step(n + 1)

        @pl.when((odd == 1) & (n < 2))
        def _():
            give_step(n + 6)

        await_bytes(comp.at[n, pl.ds(0, 4 * ROWS), :], c_core.at[n])
        for part in range(GROUP):
            rows = slice(part * ROWS, (part + 1) * ROWS)
            products = []
            for r in range(part * GROUP, (part + 1) * GROUP):
                chosen = jnp.concatenate([state[pattern[s, r]] for s in range(S)], axis=0)
                products.append(dot(comp[n, r * BS : (r + 1) * BS, :], chosen))
            wide = damp_wide[n, rows, :]
            old = state[part * GROUP : (part + 1) * GROUP].reshape(ROWS, 2 * ROWS)
            value = old.astype(F32) * jnp.concatenate([wide, wide], axis=1)
            value = value + jnp.concatenate(products, axis=0)
            mixed[rows, :] = value
            mixed_b[rows, :] = value.astype(BF16)
        quarter = STATES // 4
        seen = sum(
            dot(pick[:, q * quarter : (q + 1) * quarter], mixed_b[q * quarter : (q + 1) * quarter, :])
            for q in range(4)
        )
        lane = iota((SENSORS, ROWS), 1)
        readings = jnp.where(lane == 0, obs_wide[n], 0.0)
        seen = jnp.concatenate([seen[:, :ROWS], seen[:, ROWS:] - readings], axis=1).astype(BF16)
        for q in range(4):
            rows = slice(q * quarter, (q + 1) * quarter)
            value = mixed[rows, :] - dot(gain[rows, :], seen)
            state[q * 16 : (q + 1) * 16] = value.astype(BF16).reshape(16, BS, 2 * ROWS)
            vector_f[rows, :] = value[:, ROWS:]

        return carry

    def rows_at(m):
        return span_of(m % PARTS, CHUNK)

    def give_vector(level):
        value = vec_row[0:1, :]
        high = value.astype(BF16).astype(F32)
        row = iota((16, STATES), 0)
        both = jnp.where(
            row == 0, jnp.broadcast_to(high, (16, STATES)),
            jnp.where(row == 1, jnp.broadcast_to(value - high, (16, STATES)), 0.0),
        )
        vec_send[...] = both.astype(BF16)
        send(vec_send, vec_in.at[level], vec_sends, vec_recv.at[level], (t + SPANS[level], i))

    def give_up(level, m):
        rows = rows_at(m)
        send(
            columns_of.at[level, rows, :], earlier.at[level, rows, :],
            up_send.at[m % PARTS], up_recv.at[level * PARTS + m % PARTS], (t + SPANS[level], i),
        )

    def give_part(m):
        level = m // PARTS
        rows = rows_at(m)
        src = columns_of.at[level, rows, :]
        dst = whole.at[level, rows, own]
        send(src, dst, m_send.at[m], m_far.at[m], (t, opposite))
        send(src, dst, m_send.at[m], m_left.at[m], (t, above))
        send(src, dst, m_send.at[m], m_right.at[m], (t, below))
        send(src, dst, m_twin.at[m], m_core.at[m], (t, twin))
        whole[level, rows, own] = columns_of[level, rows, :]

    def pass_part(m):
        for p, sems in ((below, m_left), (above, m_right), (opposite, m_far)):
            part = whole.at[m // PARTS, rows_at(m), span_of(p)]
            await_bytes(part, sems.at[m])
            send(part, part, m_twin.at[m], m_core.at[m], (t, twin))

    def give_row(j):
        block = columns_of.at[merges, span_of(j), :]

        @pl.when(j != i)
        def _():
            send(block, rows_out.at[:, own], swap_send, swap_recv, (t, j))

        @pl.when(j == i)
        def _():
            rows_out[:, own] = columns_of[merges, own, :]

    def merge(m, carry):
        level = m // PARTS
        r = m % PARTS
        rows = rows_at(m)

        @pl.when(r == 0)
        def _():
            pass_part(m)

        @pl.when((level == 0) & (r == 0) & (PACE < PARTS))
        def _():
            give_part(PACE)

        @pl.when(r + 1 < PARTS)
        def _():
            pass_part(m + 1)

        @pl.when((level == 0) & (r + 1 + PACE < PARTS))
        def _():
            give_part(m + 1 + PACE)

        @pl.when(r == 0)
        def _():
            for q in range(PARTS):
                await_bytes(
                    earlier.at[level, pl.ds(q * CHUNK, CHUNK), :], up_recv.at[level * PARTS + q]
                )

        await_bytes(whole.at[level, rows, pl.ds(0, 4 * ROWS)], m_core.at[m])
        columns_of[level + 1, rows, :] = dot(whole[level, rows, :], earlier[level]).astype(BF16)

        @pl.when(level + 1 < merges)
        def _():
            give_part(m + PARTS)

        @pl.when(level + 1 == merges)
        def _():
            for d in range(CHUNK // ROWS):
                give_row(r * (CHUNK // ROWS) + d)

        for at in (1, 2):
            @pl.when(producer[at] & (level == at - 1))
            def _():
                give_up(at, m)

        @pl.when(r == PARTS - 1)
        def _():
            await_bytes(vec_in.at[level], vec_recv.at[level])
            found = lax.dot_general(
                vec_in[level], whole[level], (((1,), (1,)), ((), ())),
                preferred_element_type=F32,
            )
            vec_row[0:1, :] = vec_row[0:1, :] + found[0:1, :] + found[1:2, :]

            for at in (1, 2):
                @pl.when(producer[at] & (level == at - 1))
                def _():
                    give_vector(at)

        return carry

    @pl.when(odd == 0)
    def _():
        send(small.at[0], small.at[0], small_send, small_recv, (lead, i))
        for k in range(STRETCH):
            give_step(k)
            hand_over(k)
        pass_step(0)

    @pl.when(odd == 1)
    def _():
        give_step(STRETCH)
        give_step(STRETCH + 1)
        await_bytes(small.at[0], small_recv)
        widen(0)
        for k in range(STRETCH):
            await_bytes(piece(k, i), c_mine.at[k])
            give_step(k)
        pass_step(0)

    lax.fori_loop(0, last_step, step, 0)
    columns_of[0] = state[:, :, 0:ROWS].reshape(STATES, ROWS)

    @pl.when(merges > 0)
    def _():
        def give(m, carry):
            give_part(m)
            return carry

        lax.fori_loop(0, PACE, give, 0)

    @pl.when(producer[0])
    def _():
        for m in range(PARTS):
            give_up(0, m)

    for part in range(GROUP):
        rows = slice(part * ROWS, (part + 1) * ROWS)
        vec_row[0:1, rows] = jnp.transpose(vector_f[rows, :])[0:1, :]

    @pl.when(producer[0])
    def _():
        give_vector(0)

    @pl.when(merges == 0)
    def _():
        own_rows_out()

    lax.fori_loop(0, count, merge, 0)
    vector_out[...] = vec_row[0:1, own]

    def drained(n, carry):
        await_bytes(comp.at[n, pl.ds(0, 3 * ROWS), :], c_send.at[n])
        await_bytes(comp.at[n, pl.ds(0, 4 * ROWS), :], c_twin.at[n])
        return carry

    lax.fori_loop(0, last_step, drained, 0)

    @pl.when(odd == 0)
    def _():
        for k in range(STRETCH):
            await_bytes(piece(k, i), c_over.at[k])
        await_bytes(small.at[0], small_send)

    def drained_part(m, carry):
        rows = rows_at(m)
        await_bytes(whole.at[m // PARTS, rows, pl.ds(0, 3 * ROWS)], m_send.at[m])
        await_bytes(whole.at[m // PARTS, rows, pl.ds(0, 4 * ROWS)], m_twin.at[m])
        return carry

    lax.fori_loop(0, count, drained_part, 0)

    @pl.when(producer[0] | producer[1] | producer[2])
    def _():
        for q in range(PARTS):
            await_bytes(earlier.at[0, pl.ds(q * CHUNK, CHUNK), :], up_send.at[q])
        await_bytes(vec_send, vec_sends)

    await_bytes(rows_out.at[:, pl.ds(0, 7 * ROWS)], swap_recv)
    result = pltpu.make_async_copy(rows_out, matrix_out.at[0], out_sem)
    result.start()
    await_bytes(rows_out.at[:, pl.ds(0, 7 * ROWS)], swap_send)
    result.wait()


def shards(observations, gain, damping, blocks, pattern, sensor_index):
    anywhere = pl.BlockSpec(memory_space=pl.ANY)
    dma = pltpu.SemaphoreType.DMA
    merges = len(SPANS)
    moves = PARTS * merges
    return pl.pallas_call(
        kernel,
        out_shape=(
            jax.ShapeDtypeStruct((1, ROWS, STATES), BF16),
            jax.ShapeDtypeStruct((1, ROWS), F32),
        ),
        in_specs=[anywhere] * 6,
        out_specs=(anywhere, pl.BlockSpec(memory_space=pltpu.VMEM)),
        scratch_shapes=[
            pltpu.SMEM((S, NBLK), jnp.int32),
            pltpu.VMEM((1, SENSORS), jnp.int32),
            pltpu.VMEM((STRETCH, SENSORS), BF16),
            pltpu.VMEM((STATES, SENSORS), BF16),
            pltpu.VMEM((STRETCH, STATES), F32),
            pltpu.VMEM((STEPS, STATES, SENSORS), BF16),
            pltpu.VMEM((2, 8, STATES), F32),
            pltpu.VMEM((STEPS, STATES, ROWS), F32),
            pltpu.VMEM((STEPS, SENSORS, ROWS), F32),
            pltpu.VMEM((SENSORS, STATES), BF16),
            pltpu.VMEM((NBLK, BS, 2 * ROWS), BF16),
            pltpu.VMEM((STATES, 2 * ROWS), F32),
            pltpu.VMEM((STATES, 2 * ROWS), BF16),
            pltpu.VMEM((STATES, ROWS), F32),
            pltpu.VMEM((merges + 1, STATES, ROWS), BF16),
            pltpu.VMEM((merges, STATES, STATES), BF16),
            pltpu.VMEM((merges, STATES, ROWS), BF16),
            pltpu.VMEM((merges, 16, STATES), BF16),
            pltpu.VMEM((8, STATES), F32),
            pltpu.VMEM((16, STATES), BF16),
            pltpu.VMEM((ROWS, STATES), BF16),
            dma((6,)), dma, dma,
            *[dma((STEPS,))] * 8,
            *[dma((moves,))] * 6,
            dma((PARTS,)), dma((moves,)), dma, dma((merges,)), dma, dma, dma,
        ],
        compiler_params=pltpu.CompilerParams(
            collective_id=0, has_side_effects=True, vmem_limit_bytes=VMEM_BYTES
        ),
    )(pattern.T, sensor_index.reshape(1, SENSORS), observations, gain, damping, blocks)


def solution(mesh):
    return jax.shard_map(
        shards,
        mesh=mesh,
        in_specs=(P("tm", None), P(), P("tm", None), P("tm", "row", None), P(), P()),
        out_specs=(P("tm", "row", None), P("tm", "row")),
        check_vma=False,
    )
```

```python
import functools

import jax
import jax.numpy as jnp
from jax import lax
from jax.experimental import pallas as pl
from jax.experimental.pallas import tpu as pltpu
from jax.sharding import PartitionSpec as P

STATES = 1024
SENSORS = 128
BS = 16
S = 8
STRETCH = 4
NBLK = 64
GROUP = 8
ROWS = STATES // GROUP
STEPS = 2 * STRETCH
CHUNK = 256
PARTS = STATES // CHUNK
PACE = 4
SPANS = (2, 4, 8)
VMEM_BYTES = 63 * 2**20
MESH = pl.DeviceIdType.MESH
F32 = jnp.float32
BF16 = jnp.bfloat16


def dot(a, b):
    return jnp.dot(a, b, preferred_element_type=F32)


def iota(shape, axis):
    return lax.broadcasted_iota(jnp.int32, shape, axis)


def kernel(
    pattern_in, sensor_in, observations_in, gain_in, damping_in, blocks,
    matrix_out, vector_out,
    pattern, sensor, observations, gain, damping,
    comp, small, damp_wide, obs_wide, pick, state, mixed, mixed_b, vector_f,
    columns_of, whole, earlier, vec_in, vec_row, vec_send, rows_out,
    in_sems, small_send, small_recv,
    c_send, c_over, c_twin, c_mine, c_left, c_right, c_far, c_core,
    m_send, m_twin, m_left, m_right, m_far, m_core,
    up_send, up_recv, vec_sends, vec_recv, swap_send, swap_recv,
):
    t = lax.axis_index("tm")
    i = lax.axis_index("row")
    core = i % 2
    y = i // 2
    above = ((y + 1) % 4) * 2 + core
    below = ((y + 3) % 4) * 2 + core
    opposite = ((y + 2) % 4) * 2 + core
    twin = i + 1 - 2 * core
    odd = t % 2
    lead = t - odd + 1
    producer = [t % (2 * span) == span - 1 for span in SPANS]
    consumer = [t % (2 * span) == 2 * span - 1 for span in SPANS]
    merges = sum(c.astype(jnp.int32) for c in consumer)
    meets = sum(p.astype(jnp.int32) for p in producer)
    count = PARTS * merges

    def send(src, dst, send_sem, recv_sem, device):
        pltpu.make_async_remote_copy(
            src_ref=src, dst_ref=dst, send_sem=send_sem, recv_sem=recv_sem,
            device_id=device, device_id_type=MESH,
        ).start()

    def await_bytes(ref, sem):
        pltpu.make_async_copy(ref, ref, sem).wait()

    def span_of(p, size=ROWS):
        return pl.ds(pl.multiple_of(p * size, size), size)

    own = span_of(i)
    fetches = [
        pltpu.make_async_copy(src, dst, in_sems.at[k])
        for k, (src, dst) in enumerate(
            (
                (blocks, comp.at[pl.ds(odd * STRETCH, STRETCH), own, :]),
                (damping_in, damping), (observations_in, observations),
                (sensor_in, sensor), (pattern_in, pattern), (gain_in, gain),
            )
        )
    ]
    for fetch in fetches:
        fetch.start()
    barrier = pltpu.get_barrier_semaphore()

    def greet(device):
        pl.semaphore_signal(barrier, inc=1, device_id=device, device_id_type=MESH)

    for at, span in enumerate(SPANS):
        @pl.when(consumer[at])
        def _():
            greet((t - span, i))

    @pl.when(odd == 1)
    def _():
        greet((t - 1, i))

    for d in range(1, GROUP):
        greet((t, (i + d) % GROUP))

    def widen(b):
        columns = jnp.transpose(small[b])
        for k in range(STRETCH):
            damp_wide[b * STRETCH + k] = jnp.broadcast_to(columns[:, k : k + 1], (STATES, ROWS))
            obs_wide[b * STRETCH + k] = jnp.broadcast_to(
                columns[:SENSORS, STRETCH + k : STRETCH + k + 1], (SENSORS, ROWS)
            )

    fetches[0].wait()
    pl.semaphore_wait(barrier, GROUP - odd + meets)

    def piece(n, p):
        return comp.at[n, span_of(p), :]

    def give_step(n):
        mine = piece(n, i)
        send(mine, mine, c_twin.at[n], c_core.at[n], (t, twin))
        send(mine, mine, c_send.at[n], c_far.at[n], (t, opposite))
        send(mine, mine, c_send.at[n], c_left.at[n], (t, above))
        send(mine, mine, c_send.at[n], c_right.at[n], (t, below))

    def pass_step(n):
        for p, sems in ((below, c_left), (above, c_right), (opposite, c_far)):
            part = piece(n, p)
            await_bytes(part, sems.at[n])
            send(part, part, c_twin.at[n], c_core.at[n], (t, twin))

    def hand_over(k):
        ref = piece(k, i)
        send(ref, ref, c_over.at[k], c_mine.at[k], (lead, i))

    def own_rows_out():
        for d in (4, 5, 3, 2, 6, 7, 1):
            j = (i + d) % GROUP
            send(
                columns_of.at[0, span_of(j), :], rows_out.at[:, own], swap_send, swap_recv, (t, j)
            )
        rows_out[:, own] = columns_of[0, own, :]

    last_step = STRETCH * (1 + odd)

    def step(n, carry):
        @pl.when(n + 1 < last_step)
        def _():
            pass_step(n + 1)

        @pl.when((odd == 1) & (n < 2))
        def _():
            give_step(n + 6)

        await_bytes(comp.at[n, pl.ds(0, 4 * ROWS), :], c_core.at[n])
        for part in range(GROUP):
            rows = slice(part * ROWS, (part + 1) * ROWS)
            products = []
            for r in range(part * GROUP, (part + 1) * GROUP):
                chosen = jnp.concatenate([state[pattern[s, r]] for s in range(S)], axis=0)
                products.append(dot(comp[n, r * BS : (r + 1) * BS, :], chosen))
            wide = damp_wide[n, rows, :]
            old = state[part * GROUP : (part + 1) * GROUP].reshape(ROWS, 2 * ROWS)
            value = old.astype(F32) * jnp.concatenate([wide, wide], axis=1)
            value = value + jnp.concatenate(products, axis=0)
            mixed[rows, :] = value
            mixed_b[rows, :] = value.astype(BF16)
        quarter = STATES // 4
        seen = sum(
            dot(pick[:, q * quarter : (q + 1) * quarter], mixed_b[q * quarter : (q + 1) * quarter, :])
            for q in range(4)
        )
        lane = iota((SENSORS, ROWS), 1)
        readings = jnp.where(lane == 0, obs_wide[n], 0.0)
        seen = jnp.concatenate([seen[:, :ROWS], seen[:, ROWS:] - readings], axis=1).astype(BF16)
        for q in range(4):
            rows = slice(q * quarter, (q + 1) * quarter)
            value = mixed[rows, :] - dot(gain[rows, :], seen)
            state[q * 16 : (q + 1) * 16] = value.astype(BF16).reshape(16, BS, 2 * ROWS)
            vector_f[rows, :] = value[:, ROWS:]

        return carry

    def rows_at(m):
        return span_of(m % PARTS, CHUNK)

    def give_vector(level):
        value = vec_row[0:1, :]
        high = value.astype(BF16).astype(F32)
        row = iota((16, STATES), 0)
        both = jnp.where(
            row == 0, jnp.broadcast_to(high, (16, STATES)),
            jnp.where(row == 1, jnp.broadcast_to(value - high, (16, STATES)), 0.0),
        )
        vec_send[...] = both.astype(BF16)
        send(vec_send, vec_in.at[level], vec_sends, vec_recv.at[level], (t + SPANS[level], i))

    def give_up(level, m):
        rows = rows_at(m)
        send(
            columns_of.at[level, rows, :], earlier.at[level, rows, :],
            up_send.at[m % PARTS], up_recv.at[level * PARTS + m % PARTS], (t + SPANS[level], i),
        )

    def give_part(m):
        level = m // PARTS
        rows = rows_at(m)
        src = columns_of.at[level, rows, :]
        dst = whole.at[level, rows, own]
        send(src, dst, m_send.at[m], m_far.at[m], (t, opposite))
        send(src, dst, m_send.at[m], m_left.at[m], (t, above))
        send(src, dst, m_send.at[m], m_right.at[m], (t, below))
        send(src, dst, m_twin.at[m], m_core.at[m], (t, twin))
        whole[level, rows, own] = columns_of[level, rows, :]

    def pass_part(m):
        for p, sems in ((below, m_left), (above, m_right), (opposite, m_far)):
            part = whole.at[m // PARTS, rows_at(m), span_of(p)]
            await_bytes(part, sems.at[m])
            send(part, part, m_twin.at[m], m_core.at[m], (t, twin))

    def give_row(j):
        block = columns_of.at[merges, span_of(j), :]

        @pl.when(j != i)
        def _():
            send(block, rows_out.at[:, own], swap_send, swap_recv, (t, j))

        @pl.when(j == i)
        def _():
            rows_out[:, own] = columns_of[merges, own, :]

    def merge(m, carry):
        level = m // PARTS
        r = m % PARTS
        rows = rows_at(m)

        @pl.when(r == 0)
        def _():
            pass_part(m)

        @pl.when((level == 0) & (r == 0) & (PACE < PARTS))
        def _():
            give_part(PACE)

        @pl.when(r + 1 < PARTS)
        def _():
            pass_part(m + 1)

        @pl.when((level == 0) & (r + 1 + PACE < PARTS))
        def _():
            give_part(m + 1 + PACE)

        @pl.when(r == 0)
        def _():
            for q in range(PARTS):
                await_bytes(
                    earlier.at[level, pl.ds(q * CHUNK, CHUNK), :], up_recv.at[level * PARTS + q]
                )

        await_bytes(whole.at[level, rows, pl.ds(0, 4 * ROWS)], m_core.at[m])
        columns_of[level + 1, rows, :] = dot(whole[level, rows, :], earlier[level]).astype(BF16)

        @pl.when(level + 1 < merges)
        def _():
            give_part(m + PARTS)

        @pl.when(level + 1 == merges)
        def _():
            for d in range(CHUNK // ROWS):
                give_row(r * (CHUNK // ROWS) + d)

        for at in (1, 2):
            @pl.when(producer[at] & (level == at - 1))
            def _():
                give_up(at, m)

        @pl.when(r == PARTS - 1)
        def _():
            await_bytes(vec_in.at[level], vec_recv.at[level])
            found = lax.dot_general(
                vec_in[level], whole[level], (((1,), (1,)), ((), ())),
                preferred_element_type=F32,
            )
            vec_row[0:1, :] = vec_row[0:1, :] + found[0:1, :] + found[1:2, :]

            for at in (1, 2):
                @pl.when(producer[at] & (level == at - 1))
                def _():
                    give_vector(at)

        return carry

    @pl.when(odd == 0)
    def _():
        for k in range(STRETCH):
            give_step(k)
            hand_over(k)

    @pl.when(odd == 1)
    def _():
        give_step(STRETCH)
        give_step(STRETCH + 1)

    for fetch in fetches[1:]:
        fetch.wait()
    small[odd] = jnp.zeros((8, STATES), F32)
    small[odd, 0:STRETCH, :] = damping[...]
    small[odd, STRETCH:8, 0:SENSORS] = observations[...].astype(F32)


    @pl.when(odd == 0)
    def _():
        send(small.at[0], small.at[0], small_send, small_recv, (lead, i))

    eye = iota((SENSORS, SENSORS), 0) == iota((SENSORS, SENSORS), 1)
    sensor_col = jnp.sum(
        jnp.where(eye, jnp.broadcast_to(sensor[...].astype(F32), (SENSORS, SENSORS)), 0.0),
        axis=1, keepdims=True,
    )
    pick[...] = jnp.where(
        sensor_col == iota((SENSORS, STATES), 1).astype(F32), 1.0, 0.0
    ).astype(BF16)
    first = iota((STATES, 2 * ROWS), 0) == iota((STATES, 2 * ROWS), 1) + i * ROWS
    state[...] = jnp.where(
        first & (iota((STATES, 2 * ROWS), 1) < ROWS), 1.0, 0.0
    ).astype(BF16).reshape(NBLK, BS, 2 * ROWS)
    widen(odd)


    @pl.when(odd == 1)
    def _():
        for k in range(STRETCH):
            await_bytes(piece(k, i), c_mine.at[k])
            give_step(k)
        await_bytes(small.at[0], small_recv)
        widen(0)

    pass_step(0)
    lax.fori_loop(0, last_step, step, 0)
    columns_of[0] = state[:, :, 0:ROWS].reshape(STATES, ROWS)

    @pl.when(merges > 0)
    def _():
        def give(m, carry):
            give_part(m)
            return carry

        lax.fori_loop(0, PACE, give, 0)

    @pl.when(producer[0])
    def _():
        for m in range(PARTS):
            give_up(0, m)

    for part in range(GROUP):
        rows = slice(part * ROWS, (part + 1) * ROWS)
        vec_row[0:1, rows] = jnp.transpose(vector_f[rows, :])[0:1, :]

    @pl.when(producer[0])
    def _():
        give_vector(0)

    @pl.when(merges == 0)
    def _():
        own_rows_out()

    lax.fori_loop(0, count, merge, 0)
    vector_out[...] = vec_row[0:1, own]

    def drained(n, carry):
        await_bytes(comp.at[n, pl.ds(0, 3 * ROWS), :], c_send.at[n])
        await_bytes(comp.at[n, pl.ds(0, 4 * ROWS), :], c_twin.at[n])
        return carry

    lax.fori_loop(0, last_step, drained, 0)

    @pl.when(odd == 0)
    def _():
        for k in range(STRETCH):
            await_bytes(piece(k, i), c_over.at[k])
        await_bytes(small.at[0], small_send)

    def drained_part(m, carry):
        rows = rows_at(m)
        await_bytes(whole.at[m // PARTS, rows, pl.ds(0, 3 * ROWS)], m_send.at[m])
        await_bytes(whole.at[m // PARTS, rows, pl.ds(0, 4 * ROWS)], m_twin.at[m])
        return carry

    lax.fori_loop(0, count, drained_part, 0)

    @pl.when(producer[0] | producer[1] | producer[2])
    def _():
        for q in range(PARTS):
            await_bytes(earlier.at[0, pl.ds(q * CHUNK, CHUNK), :], up_send.at[q])
        await_bytes(vec_send, vec_sends)

    await_bytes(rows_out.at[:, pl.ds(0, 7 * ROWS)], swap_recv)
    matrix_out[0] = rows_out[...]
    await_bytes(rows_out.at[:, pl.ds(0, 7 * ROWS)], swap_send)


def shards(observations, gain, damping, blocks, pattern, sensor_index):
    anywhere = pl.BlockSpec(memory_space=pl.ANY)
    dma = pltpu.SemaphoreType.DMA
    merges = len(SPANS)
    moves = PARTS * merges
    return pl.pallas_call(
        kernel,
        out_shape=(
            pltpu.VMEM((1, ROWS, STATES), BF16),
            pltpu.VMEM((1, ROWS), F32),
        ),
        in_specs=[anywhere] * 6,
        out_specs=(pl.BlockSpec(memory_space=pltpu.VMEM),) * 2,
        scratch_shapes=[
            pltpu.SMEM((S, NBLK), jnp.int32),
            pltpu.VMEM((1, SENSORS), jnp.int32),
            pltpu.VMEM((STRETCH, SENSORS), BF16),
            pltpu.VMEM((STATES, SENSORS), BF16),
            pltpu.VMEM((STRETCH, STATES), F32),
            pltpu.VMEM((STEPS, STATES, SENSORS), BF16),
            pltpu.VMEM((2, 8, STATES), F32),
            pltpu.VMEM((STEPS, STATES, ROWS), F32),
            pltpu.VMEM((STEPS, SENSORS, ROWS), F32),
            pltpu.VMEM((SENSORS, STATES), BF16),
            pltpu.VMEM((NBLK, BS, 2 * ROWS), BF16),
            pltpu.VMEM((STATES, 2 * ROWS), F32),
            pltpu.VMEM((STATES, 2 * ROWS), BF16),
            pltpu.VMEM((STATES, ROWS), F32),
            pltpu.VMEM((merges + 1, STATES, ROWS), BF16),
            pltpu.VMEM((merges, STATES, STATES), BF16),
            pltpu.VMEM((merges, STATES, ROWS), BF16),
            pltpu.VMEM((merges, 16, STATES), BF16),
            pltpu.VMEM((8, STATES), F32),
            pltpu.VMEM((16, STATES), BF16),
            pltpu.VMEM((ROWS, STATES), BF16),
            dma((6,)), dma, dma,
            *[dma((STEPS,))] * 8,
            *[dma((moves,))] * 6,
            dma((PARTS,)), dma((moves,)), dma, dma((merges,)), dma, dma,
        ],
        compiler_params=pltpu.CompilerParams(
            collective_id=0, has_side_effects=True, vmem_limit_bytes=VMEM_BYTES
        ),
    )(pattern.T, sensor_index.reshape(1, SENSORS), observations, gain, damping, blocks)


def solution(mesh):
    return jax.shard_map(
        shards,
        mesh=mesh,
        in_specs=(P("tm", None), P(), P("tm", None), P("tm", "row", None), P(), P()),
        out_specs=(P("tm", "row", None), P("tm", "row")),
        check_vma=False,
    )
```

```python
import functools

import jax
import jax.numpy as jnp
from jax import lax
from jax.experimental import pallas as pl
from jax.experimental.pallas import tpu as pltpu
from jax.sharding import PartitionSpec as P

STATES = 1024
SENSORS = 128
BS = 16
S = 8
STRETCH = 4
NBLK = 64
GROUP = 8
ROWS = STATES // GROUP
STEPS = 2 * STRETCH
CHUNK = 256
PARTS = STATES // CHUNK
PACE = 4
SPANS = (2, 4, 8)
VMEM_BYTES = 63 * 2**20
MESH = pl.DeviceIdType.MESH
F32 = jnp.float32
BF16 = jnp.bfloat16


def dot(a, b):
    return jnp.dot(a, b, preferred_element_type=F32)


def iota(shape, axis):
    return lax.broadcasted_iota(jnp.int32, shape, axis)


def kernel(
    pattern_in, sensor_in, observations_in, gain_in, damping_in, blocks,
    matrix_out, vector_out,
    pattern, sensor, observations, gain, damping,
    comp, small, damp_wide, obs_wide, pick, state, mixed, mixed_b, vector_f,
    columns_of, whole, earlier, vec_in, vec_row, vec_send, rows_out,
    in_sems, small_send, small_recv,
    c_send, c_over, c_twin, c_mine, c_left, c_right, c_far, c_core,
    m_send, m_twin, m_left, m_right, m_far, m_core,
    up_send, up_recv, vec_sends, vec_recv, swap_send, swap_recv,
):
    t = lax.axis_index("tm")
    i = lax.axis_index("row")
    core = i % 2
    y = i // 2
    above = ((y + 1) % 4) * 2 + core
    below = ((y + 3) % 4) * 2 + core
    opposite = ((y + 2) % 4) * 2 + core
    twin = i + 1 - 2 * core
    odd = t % 2
    lead = t - odd + 1
    producer = [t % (2 * span) == span - 1 for span in SPANS]
    consumer = [t % (2 * span) == 2 * span - 1 for span in SPANS]
    merges = sum(c.astype(jnp.int32) for c in consumer)
    meets = sum(p.astype(jnp.int32) for p in producer)
    count = PARTS * merges

    def send(src, dst, send_sem, recv_sem, device):
        pltpu.make_async_remote_copy(
            src_ref=src, dst_ref=dst, send_sem=send_sem, recv_sem=recv_sem,
            device_id=device, device_id_type=MESH,
        ).start()

    def await_bytes(ref, sem):
        pltpu.make_async_copy(ref, ref, sem).wait()

    def span_of(p, size=ROWS):
        return pl.ds(pl.multiple_of(p * size, size), size)

    own = span_of(i)
    fetches = [
        pltpu.make_async_copy(src, dst, in_sems.at[k])
        for k, (src, dst) in enumerate(
            (
                (blocks, comp.at[pl.ds(odd * STRETCH, STRETCH), own, :]),
                (damping_in, damping), (observations_in, observations),
                (sensor_in, sensor), (pattern_in, pattern), (gain_in, gain),
            )
        )
    ]
    for fetch in fetches:
        fetch.start()
    barrier = pltpu.get_barrier_semaphore()

    def greet(device):
        pl.semaphore_signal(barrier, inc=1, device_id=device, device_id_type=MESH)

    for at, span in enumerate(SPANS):
        @pl.when(consumer[at])
        def _():
            greet((t - span, i))

    @pl.when(odd == 1)
    def _():
        greet((t - 1, i))

    for d in range(1, GROUP):
        greet((t, (i + d) % GROUP))

    def widen(b):
        columns = jnp.transpose(small[b])
        for k in range(STRETCH):
            damp_wide[b * STRETCH + k] = jnp.broadcast_to(columns[:, k : k + 1], (STATES, ROWS))
            obs_wide[b * STRETCH + k] = jnp.broadcast_to(
                columns[:SENSORS, STRETCH + k : STRETCH + k + 1], (SENSORS, ROWS)
            )

    fetches[0].wait()
    pl.semaphore_wait(barrier, GROUP - odd + meets)

    def piece(n, p):
        return comp.at[n, span_of(p), :]

    def give_step(n):
        mine = piece(n, i)
        send(mine, mine, c_twin.at[n], c_core.at[n], (t, twin))
        send(mine, mine, c_send.at[n], c_far.at[n], (t, opposite))
        send(mine, mine, c_send.at[n], c_left.at[n], (t, above))
        send(mine, mine, c_send.at[n], c_right.at[n], (t, below))

    def pass_step(n):
        for p, sems in ((below, c_left), (above, c_right), (opposite, c_far)):
            part = piece(n, p)
            await_bytes(part, sems.at[n])
            send(part, part, c_twin.at[n], c_core.at[n], (t, twin))

    def hand_over(k):
        ref = piece(k, i)
        send(ref, ref, c_over.at[k], c_mine.at[k], (lead, i))

    def own_rows_out():
        for d in (4, 5, 3, 2, 6, 7, 1):
            j = (i + d) % GROUP
            send(
                columns_of.at[0, span_of(j), :], rows_out.at[:, own], swap_send, swap_recv, (t, j)
            )
        rows_out[:, own] = columns_of[0, own, :]

    last_step = STRETCH * (1 + odd)

    def step(n, carry):
        @pl.when(n + 1 < last_step)
        def _():
            pass_step(n + 1)

        @pl.when((odd == 1) & (n < 3))
        def _():
            give_step(n + 5)

        await_bytes(comp.at[n, pl.ds(0, 4 * ROWS), :], c_core.at[n])
        for part in range(GROUP):
            rows = slice(part * ROWS, (part + 1) * ROWS)
            products = []
            for r in range(part * GROUP, (part + 1) * GROUP):
                chosen = jnp.concatenate([state[pattern[s, r]] for s in range(S)], axis=0)
                products.append(dot(comp[n, r * BS : (r + 1) * BS, :], chosen))
            wide = damp_wide[n, rows, :]
            old = state[part * GROUP : (part + 1) * GROUP].reshape(ROWS, 2 * ROWS)
            value = old.astype(F32) * jnp.concatenate([wide, wide], axis=1)
            value = value + jnp.concatenate(products, axis=0)
            mixed[rows, :] = value
            mixed_b[rows, :] = value.astype(BF16)
        quarter = STATES // 4
        seen = sum(
            dot(pick[:, q * quarter : (q + 1) * quarter], mixed_b[q * quarter : (q + 1) * quarter, :])
            for q in range(4)
        )
        lane = iota((SENSORS, ROWS), 1)
        readings = jnp.where(lane == 0, obs_wide[n], 0.0)
        seen = jnp.concatenate([seen[:, :ROWS], seen[:, ROWS:] - readings], axis=1).astype(BF16)
        for q in range(4):
            rows = slice(q * quarter, (q + 1) * quarter)
            value = mixed[rows, :] - dot(gain[rows, :], seen)
            state[q * 16 : (q + 1) * 16] = value.astype(BF16).reshape(16, BS, 2 * ROWS)
            vector_f[rows, :] = value[:, ROWS:]

        return carry

    def rows_at(m):
        return span_of(m % PARTS, CHUNK)

    def give_vector(level):
        value = vec_row[0:1, :]
        high = value.astype(BF16).astype(F32)
        row = iota((16, STATES), 0)
        both = jnp.where(
            row == 0, jnp.broadcast_to(high, (16, STATES)),
            jnp.where(row == 1, jnp.broadcast_to(value - high, (16, STATES)), 0.0),
        )
        vec_send[...] = both.astype(BF16)
        send(vec_send, vec_in.at[level], vec_sends, vec_recv.at[level], (t + SPANS[level], i))

    def give_up(level, m):
        rows = rows_at(m)
        send(
            columns_of.at[level, rows, :], earlier.at[level, rows, :],
            up_send.at[m % PARTS], up_recv.at[level * PARTS + m % PARTS], (t + SPANS[level], i),
        )

    def give_part(m):
        level = m // PARTS
        rows = rows_at(m)
        src = columns_of.at[level, rows, :]
        dst = whole.at[level, rows, own]
        send(src, dst, m_send.at[m], m_left.at[m], (t, above))
        send(src, dst, m_send.at[m], m_right.at[m], (t, below))
        send(src, dst, m_send.at[m], m_far.at[m], (t, opposite))
        send(src, dst, m_twin.at[m], m_core.at[m], (t, twin))
        whole[level, rows, own] = columns_of[level, rows, :]

    def pass_part(m):
        for p, sems in ((below, m_left), (above, m_right), (opposite, m_far)):
            part = whole.at[m // PARTS, rows_at(m), span_of(p)]
            await_bytes(part, sems.at[m])
            send(part, part, m_twin.at[m], m_core.at[m], (t, twin))

    def give_row(j):
        block = columns_of.at[merges, span_of(j), :]

        @pl.when(j != i)
        def _():
            send(block, rows_out.at[:, own], swap_send, swap_recv, (t, j))

        @pl.when(j == i)
        def _():
            rows_out[:, own] = columns_of[merges, own, :]

    def merge(m, carry):
        level = m // PARTS
        r = m % PARTS
        rows = rows_at(m)

        @pl.when(r == 0)
        def _():
            pass_part(m)

        @pl.when((r == 0) & (PACE < PARTS))
        def _():
            give_part(m + PACE)

        @pl.when(r + 1 < PARTS)
        def _():
            pass_part(m + 1)

        @pl.when(r + 1 + PACE < PARTS)
        def _():
            give_part(m + 1 + PACE)

        @pl.when(r == 0)
        def _():
            for q in range(PARTS):
                await_bytes(
                    earlier.at[level, pl.ds(q * CHUNK, CHUNK), :], up_recv.at[level * PARTS + q]
                )

        await_bytes(whole.at[level, rows, pl.ds(0, 4 * ROWS)], m_core.at[m])
        columns_of[level + 1, rows, :] = dot(whole[level, rows, :], earlier[level]).astype(BF16)

        @pl.when((level + 1 < merges) & (r < PACE))
        def _():
            give_part(m + PARTS)

        @pl.when(level + 1 == merges)
        def _():
            for d in range(CHUNK // ROWS):
                give_row(r * (CHUNK // ROWS) + d)

        for at in (1, 2):
            @pl.when(producer[at] & (level == at - 1))
            def _():
                give_up(at, m)

        @pl.when(r == PARTS - 1)
        def _():
            await_bytes(vec_in.at[level], vec_recv.at[level])
            found = lax.dot_general(
                vec_in[level], whole[level], (((1,), (1,)), ((), ())),
                preferred_element_type=F32,
            )
            vec_row[0:1, :] = vec_row[0:1, :] + found[0:1, :] + found[1:2, :]

            for at in (1, 2):
                @pl.when(producer[at] & (level == at - 1))
                def _():
                    give_vector(at)

        return carry

    def begin_even(k):
        hand_over(k)
        give_step(k)

    @pl.when(odd == 0)
    def _():
        begin_even(0)

    @pl.when(odd == 1)
    def _():
        give_step(STRETCH)

    for fetch in fetches[1:]:
        fetch.wait()
    small[odd] = jnp.zeros((8, STATES), F32)
    small[odd, 0:STRETCH, :] = damping[...]
    small[odd, STRETCH:8, 0:SENSORS] = observations[...].astype(F32)

    eye = iota((SENSORS, SENSORS), 0) == iota((SENSORS, SENSORS), 1)
    sensor_col = jnp.sum(
        jnp.where(eye, jnp.broadcast_to(sensor[...].astype(F32), (SENSORS, SENSORS)), 0.0),
        axis=1, keepdims=True,
    )
    pick[...] = jnp.where(
        sensor_col == iota((SENSORS, STATES), 1).astype(F32), 1.0, 0.0
    ).astype(BF16)

    @pl.when(odd == 0)
    def _():
        begin_even(1)
        send(small.at[0], small.at[0], small_send, small_recv, (lead, i))

    first = iota((STATES, 2 * ROWS), 0) == iota((STATES, 2 * ROWS), 1) + i * ROWS
    state[...] = jnp.where(
        first & (iota((STATES, 2 * ROWS), 1) < ROWS), 1.0, 0.0
    ).astype(BF16).reshape(NBLK, BS, 2 * ROWS)

    @pl.when(odd == 0)
    def _():
        begin_even(2)

    widen(odd)

    @pl.when(odd == 0)
    def _():
        begin_even(3)

    @pl.when(odd == 1)
    def _():
        for k in range(STRETCH):
            await_bytes(piece(k, i), c_mine.at[k])
            give_step(k)
        await_bytes(small.at[0], small_recv)
        widen(0)

    pass_step(0)
    lax.fori_loop(0, last_step, step, 0)
    columns_of[0] = state[:, :, 0:ROWS].reshape(STATES, ROWS)

    @pl.when(merges > 0)
    def _():
        def give(m, carry):
            give_part(m)
            return carry

        lax.fori_loop(0, PACE, give, 0)

    @pl.when(producer[0])
    def _():
        for m in range(PARTS):
            give_up(0, m)

    for part in range(GROUP):
        rows = slice(part * ROWS, (part + 1) * ROWS)
        vec_row[0:1, rows] = jnp.transpose(vector_f[rows, :])[0:1, :]

    @pl.when(producer[0])
    def _():
        give_vector(0)

    @pl.when(merges == 0)
    def _():
        own_rows_out()

    lax.fori_loop(0, count, merge, 0)
    vector_out[...] = vec_row[0:1, own]

    def drained(n, carry):
        await_bytes(comp.at[n, pl.ds(0, 3 * ROWS), :], c_send.at[n])
        await_bytes(comp.at[n, pl.ds(0, 4 * ROWS), :], c_twin.at[n])
        return carry

    lax.fori_loop(0, last_step, drained, 0)

    @pl.when(odd == 0)
    def _():
        for k in range(STRETCH):
            await_bytes(piece(k, i), c_over.at[k])
        await_bytes(small.at[0], small_send)

    def drained_part(m, carry):
        rows = rows_at(m)
        await_bytes(whole.at[m // PARTS, rows, pl.ds(0, 3 * ROWS)], m_send.at[m])
        await_bytes(whole.at[m // PARTS, rows, pl.ds(0, 4 * ROWS)], m_twin.at[m])
        return carry

    lax.fori_loop(0, count, drained_part, 0)

    @pl.when(producer[0] | producer[1] | producer[2])
    def _():
        for q in range(PARTS):
            await_bytes(earlier.at[0, pl.ds(q * CHUNK, CHUNK), :], up_send.at[q])
        await_bytes(vec_send, vec_sends)

    await_bytes(rows_out.at[:, pl.ds(0, 7 * ROWS)], swap_recv)
    matrix_out[0] = rows_out[...]
    await_bytes(rows_out.at[:, pl.ds(0, 7 * ROWS)], swap_send)


def shards(observations, gain, damping, blocks, pattern, sensor_index):
    anywhere = pl.BlockSpec(memory_space=pl.ANY)
    dma = pltpu.SemaphoreType.DMA
    merges = len(SPANS)
    moves = PARTS * merges
    return pl.pallas_call(
        kernel,
        out_shape=(
            pltpu.VMEM((1, ROWS, STATES), BF16),
            pltpu.VMEM((1, ROWS), F32),
        ),
        in_specs=[anywhere] * 6,
        out_specs=(pl.BlockSpec(memory_space=pltpu.VMEM),) * 2,
        scratch_shapes=[
            pltpu.SMEM((S, NBLK), jnp.int32),
            pltpu.VMEM((1, SENSORS), jnp.int32),
            pltpu.VMEM((STRETCH, SENSORS), BF16),
            pltpu.VMEM((STATES, SENSORS), BF16),
            pltpu.VMEM((STRETCH, STATES), F32),
            pltpu.VMEM((STEPS, STATES, SENSORS), BF16),
            pltpu.VMEM((2, 8, STATES), F32),
            pltpu.VMEM((STEPS, STATES, ROWS), F32),
            pltpu.VMEM((STEPS, SENSORS, ROWS), F32),
            pltpu.VMEM((SENSORS, STATES), BF16),
            pltpu.VMEM((NBLK, BS, 2 * ROWS), BF16),
            pltpu.VMEM((STATES, 2 * ROWS), F32),
            pltpu.VMEM((STATES, 2 * ROWS), BF16),
            pltpu.VMEM((STATES, ROWS), F32),
            pltpu.VMEM((merges + 1, STATES, ROWS), BF16),
            pltpu.VMEM((merges, STATES, STATES), BF16),
            pltpu.VMEM((merges, STATES, ROWS), BF16),
            pltpu.VMEM((merges, 16, STATES), BF16),
            pltpu.VMEM((8, STATES), F32),
            pltpu.VMEM((16, STATES), BF16),
            pltpu.VMEM((ROWS, STATES), BF16),
            dma((6,)), dma, dma,
            *[dma((STEPS,))] * 8,
            *[dma((moves,))] * 6,
            dma((PARTS,)), dma((moves,)), dma, dma((merges,)), dma, dma,
        ],
        compiler_params=pltpu.CompilerParams(
            collective_id=0, has_side_effects=True, vmem_limit_bytes=VMEM_BYTES
        ),
    )(pattern.T, sensor_index.reshape(1, SENSORS), observations, gain, damping, blocks)


def solution(mesh):
    return jax.shard_map(
        shards,
        mesh=mesh,
        in_specs=(P("tm", None), P(), P("tm", None), P("tm", "row", None), P(), P()),
        out_specs=(P("tm", "row", None), P("tm", "row")),
        check_vma=False,
    )
```

```python
import functools

import jax
import jax.numpy as jnp
from jax import lax
from jax.experimental import pallas as pl
from jax.experimental.pallas import tpu as pltpu
from jax.sharding import PartitionSpec as P

STATES = 1024
SENSORS = 128
BS = 16
S = 8
STRETCH = 4
NBLK = 64
GROUP = 8
ROWS = STATES // GROUP
STEPS = 2 * STRETCH
CHUNK = 256
PARTS = STATES // CHUNK
PACE = 4
SPANS = (2, 4, 8)
VMEM_BYTES = 63 * 2**20
MESH = pl.DeviceIdType.MESH
F32 = jnp.float32
BF16 = jnp.bfloat16


def dot(a, b):
    return jnp.dot(a, b, preferred_element_type=F32)


def iota(shape, axis):
    return lax.broadcasted_iota(jnp.int32, shape, axis)


def kernel(
    pattern_in, sensor_in, observations_in, gain_in, damping_in, blocks,
    matrix_out, vector_out,
    pattern, sensor, observations, gain, damping,
    comp, small, damp_wide, obs_wide, pick, state, mixed, mixed_b, vector_f,
    columns_of, whole, earlier, vec_in, vec_row, vec_send, rows_out,
    in_sems, small_send, small_recv,
    c_send, c_over, c_twin, c_mine, c_left, c_right, c_far, c_core,
    m_send, m_twin, m_left, m_right, m_far, m_core,
    up_send, up_recv, vec_sends, vec_recv, swap_send, swap_recv,
):
    t = lax.axis_index("tm")
    i = lax.axis_index("row")
    core = i % 2
    y = i // 2
    above = ((y + 1) % 4) * 2 + core
    below = ((y + 3) % 4) * 2 + core
    opposite = ((y + 2) % 4) * 2 + core
    twin = i + 1 - 2 * core
    odd = t % 2
    lead = t - odd + 1
    producer = [t % (2 * span) == span - 1 for span in SPANS]
    consumer = [t % (2 * span) == 2 * span - 1 for span in SPANS]
    merges = sum(c.astype(jnp.int32) for c in consumer)
    meets = sum(p.astype(jnp.int32) for p in producer)
    count = PARTS * merges

    def send(src, dst, send_sem, recv_sem, device):
        pltpu.make_async_remote_copy(
            src_ref=src, dst_ref=dst, send_sem=send_sem, recv_sem=recv_sem,
            device_id=device, device_id_type=MESH,
        ).start()

    def await_bytes(ref, sem):
        pltpu.make_async_copy(ref, ref, sem).wait()

    def span_of(p, size=ROWS):
        return pl.ds(pl.multiple_of(p * size, size), size)

    own = span_of(i)
    fetches = [
        pltpu.make_async_copy(src, dst, in_sems.at[k])
        for k, (src, dst) in enumerate(
            (
                (blocks, comp.at[pl.ds(odd * STRETCH, STRETCH), own, :]),
                (damping_in, damping), (observations_in, observations),
                (sensor_in, sensor), (pattern_in, pattern), (gain_in, gain),
            )
        )
    ]
    for fetch in fetches:
        fetch.start()
    barrier = pltpu.get_barrier_semaphore()

    def greet(device):
        pl.semaphore_signal(barrier, inc=1, device_id=device, device_id_type=MESH)

    for at, span in enumerate(SPANS):
        @pl.when(consumer[at])
        def _():
            greet((t - span, i))

    @pl.when(odd == 1)
    def _():
        greet((t - 1, i))

    for d in range(1, GROUP):
        greet((t, (i + d) % GROUP))

    def widen(b):
        columns = jnp.transpose(small[b])
        for k in range(STRETCH):
            damp_wide[b * STRETCH + k] = jnp.broadcast_to(columns[:, k : k + 1], (STATES, ROWS))
            obs_wide[b * STRETCH + k] = jnp.broadcast_to(
                columns[:SENSORS, STRETCH + k : STRETCH + k + 1], (SENSORS, ROWS)
            )

    fetches[0].wait()
    pl.semaphore_wait(barrier, GROUP - odd + meets)

    def piece(n, p):
        return comp.at[n, span_of(p), :]

    def give_step(n):
        mine = piece(n, i)
        send(mine, mine, c_twin.at[n], c_core.at[n], (t, twin))
        send(mine, mine, c_send.at[n], c_far.at[n], (t, opposite))
        send(mine, mine, c_send.at[n], c_left.at[n], (t, above))
        send(mine, mine, c_send.at[n], c_right.at[n], (t, below))

    def pass_step(n):
        for p, sems in ((below, c_left), (above, c_right), (opposite, c_far)):
            part = piece(n, p)
            await_bytes(part, sems.at[n])
            send(part, part, c_twin.at[n], c_core.at[n], (t, twin))

    def hand_over(k):
        ref = piece(k, i)
        send(ref, ref, c_over.at[k], c_mine.at[k], (lead, i))

    def own_rows_out():
        for d in (4, 5, 3, 2, 6, 7, 1):
            j = (i + d) % GROUP
            send(
                columns_of.at[0, span_of(j), :], rows_out.at[:, own], swap_send, swap_recv, (t, j)
            )
        rows_out[:, own] = columns_of[0, own, :]

    last_step = STRETCH * (1 + odd)

    def step(n, carry):
        @pl.when(n + 1 < last_step)
        def _():
            pass_step(n + 1)

        @pl.when((odd == 1) & (n < 3))
        def _():
            give_step(n + 5)

        await_bytes(comp.at[n, pl.ds(0, 4 * ROWS), :], c_core.at[n])
        for part in range(GROUP):
            rows = slice(part * ROWS, (part + 1) * ROWS)
            products = []
            for r in range(part * GROUP, (part + 1) * GROUP):
                chosen = jnp.concatenate([state[pattern[s, r]] for s in range(S)], axis=0)
                products.append(dot(comp[n, r * BS : (r + 1) * BS, :], chosen))
            wide = damp_wide[n, rows, :]
            old = state[part * GROUP : (part + 1) * GROUP].reshape(ROWS, 2 * ROWS)
            value = old.astype(F32) * jnp.concatenate([wide, wide], axis=1)
            value = value + jnp.concatenate(products, axis=0)
            mixed[rows, :] = value
            mixed_b[rows, :] = value.astype(BF16)
        quarter = STATES // 4
        seen = sum(
            dot(pick[:, q * quarter : (q + 1) * quarter], mixed_b[q * quarter : (q + 1) * quarter, :])
            for q in range(4)
        )
        lane = iota((SENSORS, ROWS), 1)
        readings = jnp.where(lane == 0, obs_wide[n], 0.0)
        seen = jnp.concatenate([seen[:, :ROWS], seen[:, ROWS:] - readings], axis=1).astype(BF16)
        for q in range(4):
            rows = slice(q * quarter, (q + 1) * quarter)
            value = mixed[rows, :] - dot(gain[rows, :], seen)
            state[q * 16 : (q + 1) * 16] = value.astype(BF16).reshape(16, BS, 2 * ROWS)
            vector_f[rows, :] = value[:, ROWS:]

        return carry

    def rows_at(m):
        return span_of(m % PARTS, CHUNK)

    def give_vector(level):
        value = vec_row[0:1, :]
        high = value.astype(BF16).astype(F32)
        row = iota((16, STATES), 0)
        both = jnp.where(
            row == 0, jnp.broadcast_to(high, (16, STATES)),
            jnp.where(row == 1, jnp.broadcast_to(value - high, (16, STATES)), 0.0),
        )
        vec_send[...] = both.astype(BF16)
        send(vec_send, vec_in.at[level], vec_sends, vec_recv.at[level], (t + SPANS[level], i))

    def give_up(level, m):
        rows = rows_at(m)
        send(
            columns_of.at[level, rows, :], earlier.at[level, rows, :],
            up_send.at[m % PARTS], up_recv.at[level * PARTS + m % PARTS], (t + SPANS[level], i),
        )

    def give_part(m):
        level = m // PARTS
        rows = rows_at(m)
        src = columns_of.at[level, rows, :]
        dst = whole.at[level, rows, own]
        send(src, dst, m_twin.at[m], m_core.at[m], (t, twin))
        send(src, dst, m_send.at[m], m_left.at[m], (t, above))
        send(src, dst, m_send.at[m], m_right.at[m], (t, below))
        send(src, dst, m_send.at[m], m_far.at[m], (t, opposite))
        whole[level, rows, own] = columns_of[level, rows, :]

    def pass_part(m):
        for p, sems in ((below, m_left), (above, m_right), (opposite, m_far)):
            part = whole.at[m // PARTS, rows_at(m), span_of(p)]
            await_bytes(part, sems.at[m])
            send(part, part, m_twin.at[m], m_core.at[m], (t, twin))

    def give_row(j):
        block = columns_of.at[merges, span_of(j), :]

        @pl.when(j != i)
        def _():
            send(block, rows_out.at[:, own], swap_send, swap_recv, (t, j))

        @pl.when(j == i)
        def _():
            rows_out[:, own] = columns_of[merges, own, :]

    def merge(m, carry):
        level = m // PARTS
        r = m % PARTS
        rows = rows_at(m)

        @pl.when(r == 0)
        def _():
            pass_part(m)

        @pl.when((r == 0) & (PACE < PARTS))
        def _():
            give_part(m + PACE)

        @pl.when(r + 1 < PARTS)
        def _():
            pass_part(m + 1)

        @pl.when(r + 1 + PACE < PARTS)
        def _():
            give_part(m + 1 + PACE)

        @pl.when(r == 0)
        def _():
            for q in range(PARTS):
                await_bytes(
                    earlier.at[level, pl.ds(q * CHUNK, CHUNK), :], up_recv.at[level * PARTS + q]
                )

        await_bytes(whole.at[level, rows, pl.ds(0, 4 * ROWS)], m_core.at[m])
        columns_of[level + 1, rows, :] = dot(whole[level, rows, :], earlier[level]).astype(BF16)

        @pl.when((level + 1 < merges) & (r < PACE))
        def _():
            give_part(m + PARTS)

        @pl.when(level + 1 == merges)
        def _():
            for d in range(CHUNK // ROWS):
                give_row(r * (CHUNK // ROWS) + d)

        for at in (1, 2):
            @pl.when(producer[at] & (level == at - 1))
            def _():
                give_up(at, m)

        @pl.when(r == PARTS - 1)
        def _():
            await_bytes(vec_in.at[level], vec_recv.at[level])
            found = lax.dot_general(
                vec_in[level], whole[level], (((1,), (1,)), ((), ())),
                preferred_element_type=F32,
            )
            vec_row[0:1, :] = vec_row[0:1, :] + found[0:1, :] + found[1:2, :]

            for at in (1, 2):
                @pl.when(producer[at] & (level == at - 1))
                def _():
                    give_vector(at)

        return carry

    def begin_even(k):
        hand_over(k)
        give_step(k)

    @pl.when(odd == 0)
    def _():
        begin_even(0)

    @pl.when(odd == 1)
    def _():
        give_step(STRETCH)

    for fetch in fetches[1:]:
        fetch.wait()
    small[odd] = jnp.zeros((8, STATES), F32)
    small[odd, 0:STRETCH, :] = damping[...]
    small[odd, STRETCH:8, 0:SENSORS] = observations[...].astype(F32)

    eye = iota((SENSORS, SENSORS), 0) == iota((SENSORS, SENSORS), 1)
    sensor_col = jnp.sum(
        jnp.where(eye, jnp.broadcast_to(sensor[...].astype(F32), (SENSORS, SENSORS)), 0.0),
        axis=1, keepdims=True,
    )
    pick[...] = jnp.where(
        sensor_col == iota((SENSORS, STATES), 1).astype(F32), 1.0, 0.0
    ).astype(BF16)

    @pl.when(odd == 0)
    def _():
        begin_even(1)
        send(small.at[0], small.at[0], small_send, small_recv, (lead, i))

    first = iota((STATES, 2 * ROWS), 0) == iota((STATES, 2 * ROWS), 1) + i * ROWS
    state[...] = jnp.where(
        first & (iota((STATES, 2 * ROWS), 1) < ROWS), 1.0, 0.0
    ).astype(BF16).reshape(NBLK, BS, 2 * ROWS)

    @pl.when(odd == 0)
    def _():
        begin_even(2)

    widen(odd)

    @pl.when(odd == 0)
    def _():
        begin_even(3)

    @pl.when(odd == 1)
    def _():
        for k in range(STRETCH):
            await_bytes(piece(k, i), c_mine.at[k])
            give_step(k)
        await_bytes(small.at[0], small_recv)
        widen(0)

    pass_step(0)
    lax.fori_loop(0, last_step, step, 0)
    columns_of[0] = state[:, :, 0:ROWS].reshape(STATES, ROWS)

    @pl.when(merges > 0)
    def _():
        def give(m, carry):
            give_part(m)
            return carry

        lax.fori_loop(0, PACE, give, 0)

    @pl.when(producer[0])
    def _():
        for m in range(PARTS):
            give_up(0, m)

    for part in range(GROUP):
        rows = slice(part * ROWS, (part + 1) * ROWS)
        vec_row[0:1, rows] = jnp.transpose(vector_f[rows, :])[0:1, :]

    @pl.when(producer[0])
    def _():
        give_vector(0)

    @pl.when(merges == 0)
    def _():
        own_rows_out()

    lax.fori_loop(0, count, merge, 0)
    vector_out[...] = vec_row[0:1, own]

    def drained(n, carry):
        await_bytes(comp.at[n, pl.ds(0, 3 * ROWS), :], c_send.at[n])
        await_bytes(comp.at[n, pl.ds(0, 4 * ROWS), :], c_twin.at[n])
        return carry

    lax.fori_loop(0, last_step, drained, 0)

    @pl.when(odd == 0)
    def _():
        for k in range(STRETCH):
            await_bytes(piece(k, i), c_over.at[k])
        await_bytes(small.at[0], small_send)

    def drained_part(m, carry):
        rows = rows_at(m)
        await_bytes(whole.at[m // PARTS, rows, pl.ds(0, 3 * ROWS)], m_send.at[m])
        await_bytes(whole.at[m // PARTS, rows, pl.ds(0, 4 * ROWS)], m_twin.at[m])
        return carry

    lax.fori_loop(0, count, drained_part, 0)

    @pl.when(producer[0] | producer[1] | producer[2])
    def _():
        for q in range(PARTS):
            await_bytes(earlier.at[0, pl.ds(q * CHUNK, CHUNK), :], up_send.at[q])
        await_bytes(vec_send, vec_sends)

    await_bytes(rows_out.at[:, pl.ds(0, 7 * ROWS)], swap_recv)
    matrix_out[0] = rows_out[...]
    await_bytes(rows_out.at[:, pl.ds(0, 7 * ROWS)], swap_send)


def shards(observations, gain, damping, blocks, pattern, sensor_index):
    anywhere = pl.BlockSpec(memory_space=pl.ANY)
    dma = pltpu.SemaphoreType.DMA
    merges = len(SPANS)
    moves = PARTS * merges
    return pl.pallas_call(
        kernel,
        out_shape=(
            pltpu.VMEM((1, ROWS, STATES), BF16),
            pltpu.VMEM((1, ROWS), F32),
        ),
        in_specs=[anywhere] * 6,
        out_specs=(pl.BlockSpec(memory_space=pltpu.VMEM),) * 2,
        scratch_shapes=[
            pltpu.SMEM((S, NBLK), jnp.int32),
            pltpu.VMEM((1, SENSORS), jnp.int32),
            pltpu.VMEM((STRETCH, SENSORS), BF16),
            pltpu.VMEM((STATES, SENSORS), BF16),
            pltpu.VMEM((STRETCH, STATES), F32),
            pltpu.VMEM((STEPS, STATES, SENSORS), BF16),
            pltpu.VMEM((2, 8, STATES), F32),
            pltpu.VMEM((STEPS, STATES, ROWS), F32),
            pltpu.VMEM((STEPS, SENSORS, ROWS), F32),
            pltpu.VMEM((SENSORS, STATES), BF16),
            pltpu.VMEM((NBLK, BS, 2 * ROWS), BF16),
            pltpu.VMEM((STATES, 2 * ROWS), F32),
            pltpu.VMEM((STATES, 2 * ROWS), BF16),
            pltpu.VMEM((STATES, ROWS), F32),
            pltpu.VMEM((merges + 1, STATES, ROWS), BF16),
            pltpu.VMEM((merges, STATES, STATES), BF16),
            pltpu.VMEM((merges, STATES, ROWS), BF16),
            pltpu.VMEM((merges, 16, STATES), BF16),
            pltpu.VMEM((8, STATES), F32),
            pltpu.VMEM((16, STATES), BF16),
            pltpu.VMEM((ROWS, STATES), BF16),
            dma((6,)), dma, dma,
            *[dma((STEPS,))] * 8,
            *[dma((moves,))] * 6,
            dma((PARTS,)), dma((moves,)), dma, dma((merges,)), dma, dma,
        ],
        compiler_params=pltpu.CompilerParams(
            collective_id=0, has_side_effects=True, vmem_limit_bytes=VMEM_BYTES
        ),
    )(pattern.T, sensor_index.reshape(1, SENSORS), observations, gain, damping, blocks)


def solution(mesh):
    return jax.shard_map(
        shards,
        mesh=mesh,
        in_specs=(P("tm", None), P(), P("tm", None), P("tm", "row", None), P(), P()),
        out_specs=(P("tm", "row", None), P("tm", "row")),
        check_vma=False,
    )
```
